128 devices in a mesh: gx: 8 (over y, core), gy: 16 (over z, x).
Axes of the slice: x: 4, y: 4, z: 4, core: 2. Of those that a mesh axis runs over, the one named last changes fastest.
Arguments:
- rhs_matrix: float32 [2048, 2048], P('gx', 'gy'), may hold values from -6 to 6
- trans_x: float32 [2048, 2048], P('gx', 'gy'), may hold values from 0.2 to 5
- trans_y: float32 [2048, 2048], P('gx', 'gy'), may hold values from 0.2 to 5
- leak_matrix: float32 [2048, 2048], P('gx', 'gy'), may hold values from 0.02 to 0.2
- rhs_fracture: float32 [16384, 128], P(('gx', 'gy')), may hold values from -6 to 6
- trans_frac: float32 [16384, 128], P(('gx', 'gy')), may hold values from 2 to 50
- store_frac: float32 [16384, 128], P(('gx', 'gy')), may hold values from 0.05 to 0.5
- mortar_coef: float32 [16384, 128], P(('gx', 'gy')), may hold values from 0.2 to 5
- block_home: int32 [16384, 1], P(('gx', 'gy')), may hold values from 0 to 127; in each aligned block of 128 rows (0 to 127, 128 to 255, ...) at most 2 rows name the same one
- block_len: int32 [16384], P(('gx', 'gy')), may hold values from 1 to 128, 1572864 in all
- mortar_cell: int32 [16384, 1], P(('gx', 'gy')), may hold values from 0 to 63
- cross_cell: int32 [16384, 2], P(('gx', 'gy')), may hold values from 0 to 127
- cross_partner: int32 [16384, 2], P(('gx', 'gy')), may hold values from 0 to 16383
- cross_trans: float32 [16384, 2], P(('gx', 'gy')), may hold values from 0.5 to 5
Outputs:
- pressure_matrix: float32 [2048, 2048], P('gx', 'gy')
- pressure_fracture: float32 [16384, 128], P(('gx', 'gy'))
- mortar_flux: float32 [16384, 128], P(('gx', 'gy'))
The draws below stay inside these ranges and needn't reach their ends.
Inputs may be any that keep to these rules, and one draw needn't show every extreme that they name: `block_home`: among the 128 blocks stored on one device (aligned blocks of rows), no tile is named more than 2 times, a bound that some block reaches. Tile t holds grid rows 256 * (t // 16) onward and grid columns 128 * (t % 16) onward. Cells c >= block_len[b] of block b are padding. `mortar_cell`: segment m covers row m of the home tile, all of its 128 columns; the fractures cross the first 64 rows of a tile. `cross_partner`: index k * 128 + c of cell c of the k-th block of the group of 128 blocks b // 128 that holds block b.
All inputs are finite; a program needn't handle non-finite values.
Results may differ from the reference program's by a relative error of at most 0.00012.
Values sent between devices are 32-bit elements; how exact they have to be, the bound alone decides.
A program may use at most 64 MiB of HBM per device.

```python
import math
import jax
import jax.numpy as jnp
import numpy as np
from jax import lax

CX = 256
CY = 128
BLK_DEV = 128
FBS = 128
NINT = 2
ITERS = 3
CAP = 2
NX = 2048
NY = 2048
NBLK = 16384
N_GY = 16
DEVICES = 128


def place_ends(values, stream_key, smallest, top_value):
    place = [jax.random.randint(jax.random.fold_in(stream_key, axis), (), 0, length) for axis, length in enumerate(values.shape)]
    main_axis = values.shape.index(max(values.shape))
    neighbour = place[:main_axis] + [(place[main_axis] + 1) % values.shape[main_axis]] + place[main_axis + 1:]
    return values.at[tuple(place)].set(smallest).at[tuple(neighbour)].set(top_value)


def block_scale(rng, extent, cuts, low, top_value):
    def one(dim, parts):
        draws = jax.random.uniform(jax.random.fold_in(jax.random.fold_in(rng, 6), dim), (parts,), jnp.float32, low / len(cuts), top_value / len(cuts))
        return jnp.repeat(jnp.exp(draws), extent[dim] // parts).reshape((-1,) + (1,) * (len(extent) - dim - 1))

    loudness = one(*cuts[0])
    for cut in cuts[1:]:
        loudness = loudness * one(*cut)
    return loudness


def profile(number_of, total, bound, slope):
    weights = [(1 << 20) // math.isqrt(rank ** slope) + 1 for rank in range(2, number_of + 1)]
    rest, given = total - bound - (number_of - 1), [1] * (number_of - 1)
    while rest > 0:
        free = [i for i in range(number_of - 1) if given[i] < bound]
        whole, remaining = sum([weights[i] for i in free]), rest
        for i in free:
            extra = min(bound - given[i], max(1, remaining * weights[i] // whole), rest)
            given[i] = given[i] + extra
            rest = rest - extra
    return np.array([bound] + given)


def uneven(key, number_of, total, bound, lean):
    if number_of == 2:
        one = jax.random.randint(key, (), max(1, total - bound), min(bound, total - 1) + 1)
        return jnp.stack([one, total - one])
    sizes = jnp.asarray(profile(number_of, total, bound, lean), jnp.int32)
    couples = (number_of - 1) // 2
    source_of, receiver = sizes[1:1 + 2 * couples:2], sizes[2:2 + 2 * couples:2]
    room = jnp.minimum(source_of - 1, bound - receiver)
    passed = jax.random.randint(jax.random.fold_in(key, 1), (couples,), 0, 1 << 20) % (room + 1)
    sizes = sizes.at[1:1 + 2 * couples:2].set(source_of - passed).at[2:2 + 2 * couples:2].set(receiver + passed)
    return sizes[jax.random.permutation(jax.random.fold_in(key, 2), number_of)]


def deal_out(own_key, own, number, rows, count, top, bound, lean):
    sequence = jax.random.permutation(own_key, count)
    packed, usual = load_shares(count, rows * top, bound, lean, True), load_shares(count, rows * top, bound, lean, False)
    places = jnp.arange(count)

    def named(lengths, turn):
        used = int((lengths > 0).sum())
        fixed = max(1, used // 4)
        passed = fixed + (places - fixed + turn * (used - fixed)) % max(1, count - fixed)
        return jnp.zeros((count,), jnp.int32).at[sequence[jnp.where(places < fixed, places, passed)]].set(jnp.asarray(lengths, jnp.int32))

    lengths = jnp.where(number % 4 == 0, named(packed, number // 4), named(usual, number - number // 4 - 1))
    mixed = jax.random.permutation(jax.random.fold_in(own, 3), count)
    donor, receiver = mixed[0:count // 2 * 2:2], mixed[1:count // 2 * 2:2]
    margin = jnp.minimum(lengths[donor] - 1, bound - lengths[receiver]) // 2
    margin = jnp.where((donor == sequence[0]) | (receiver == sequence[0]) | (lengths[receiver] == 0), 0, jnp.maximum(margin, 0))
    passed = jax.random.randint(jax.random.fold_in(own, 4), (count // 2,), 0, 1 << 20) % (margin + 1)
    lengths = lengths.at[donor].add(-passed).at[receiver].add(passed)
    items = jnp.searchsorted(jnp.cumsum(lengths), jnp.arange(rows * top), side="right").astype(jnp.int32)
    grid = items.reshape(top, rows).T
    grid = grid[jax.random.permutation(jax.random.fold_in(own, 1), rows)]
    turn = jax.random.randint(jax.random.fold_in(own, 2), (rows, 1), 0, top)
    return jnp.take_along_axis(grid, (jnp.arange(top)[None, :] + turn) % top, axis=1)


def load_shares(count, total, reach, skew, full):
    loads = [(1 << 20) // math.isqrt(rank ** skew) + 1 for rank in range(1, count + 1)]
    largest = reach if full else min(reach, max(-(-total // count), total * loads[0] // sum(loads)))
    least = 1 if total - largest >= count - 1 else 0
    holding, surplus = [largest] + [least] * (count - 1), total - largest - least * (count - 1)
    while surplus > 0:
        candidates = [i for i in range(1, count) if holding[i] < largest] or [i for i in range(1, count) if holding[i] < reach]
        mass, budget = sum([loads[i] for i in candidates]), surplus
        for i in candidates:
            more = min(reach - holding[i], max(1, budget * loads[i] // mass), surplus)
            holding[i] = holding[i] + more
            surplus = surplus - more
    return np.array(holding)


def bell_draw(own_key, shape, width, most, cuts=(), dtype=jnp.bfloat16):
    loudness = block_scale(own_key, shape, cuts, -0.22, 0.18) if cuts else 1.0
    values = jax.random.normal(own_key, shape, jnp.float32) * width * loudness
    return jnp.minimum(jnp.maximum(values, -most), most).astype(dtype)


def setup_inputs(seed: int = 0) -> dict:
    seeds = jax.random.split(jax.random.key(seed), 15)
    rhs_matrix = bell_draw(seeds[0], (NX, NY), 1.0, 6.0, ((0, 8), (1, 16)), jnp.float32)
    trans_x = jnp.clip(jnp.exp(math.log(5.0) - 3.218876 * jax.random.uniform(seeds[1], (NX, NY), jnp.float32) ** block_scale(seeds[1], (NX, NY), ((0, 8), (1, 16)), -0.2, 0.2)), 0.2, 5.0)
    trans_y = jnp.clip(jnp.exp(math.log(5.0) - 3.218876 * jax.random.uniform(seeds[2], (NX, NY), jnp.float32) ** block_scale(seeds[2], (NX, NY), ((0, 8), (1, 16)), -0.2, 0.2)), 0.2, 5.0)
    leak_matrix = jnp.clip(jnp.exp(math.log(0.2) - 2.3025851 * jax.random.uniform(seeds[3], (NX, NY), jnp.float32) ** block_scale(seeds[3], (NX, NY), ((0, 8), (1, 16)), -0.2, 0.2)), 0.02, 0.2)
    rhs_fracture = bell_draw(seeds[4], (NBLK, FBS), 1.0, 6.0, ((0, 128),), jnp.float32)
    trans_frac = jnp.clip(jnp.exp(math.log(50.0) - 3.218876 * jax.random.uniform(seeds[5], (NBLK, FBS), jnp.float32) ** block_scale(seeds[5], (NBLK, FBS), ((0, 128),), -0.2, 0.2)), 2.0, 50.0)
    store_frac = jnp.clip(jnp.exp(math.log(0.5) - 2.3025851 * jax.random.uniform(seeds[6], (NBLK, FBS), jnp.float32) ** block_scale(seeds[6], (NBLK, FBS), ((0, 128),), -0.2, 0.2)), 0.05, 0.5)
    mortar_coef = jnp.clip(jnp.exp(math.log(5.0) - 3.218876 * jax.random.uniform(seeds[7], (NBLK, FBS), jnp.float32) ** block_scale(seeds[7], (NBLK, FBS), ((0, 128),), -0.2, 0.2)), 0.2, 5.0)
    block_home_keys = jax.random.split(jax.random.fold_in(seeds[8], 1), NBLK // BLK_DEV)
    block_home_turns = jax.random.permutation(jax.random.fold_in(seeds[8], 3), NBLK // BLK_DEV)
    block_home = jax.vmap(lambda own, number: deal_out(jax.random.fold_in(seeds[8], 2), own, number, BLK_DEV, DEVICES, 1, CAP, 2))(block_home_keys, block_home_turns).reshape((NBLK, 1))
    block_len = uneven(seeds[9], NBLK, NBLK * FBS * 3 // 4, FBS, 1).astype(jnp.int32)
    mortar_cell = place_ends(jax.random.randint(seeds[10], (NBLK, 1), 0, (CX // 4) * (CY // FBS)), jax.random.fold_in(seeds[10], 1), 0, ((CX // 4) * (CY // FBS)) - 1).astype(jnp.int32)
    cross_cell = place_ends(jax.random.randint(seeds[11], (NBLK, NINT), 0, FBS), jax.random.fold_in(seeds[11], 1), 0, FBS - 1).astype(jnp.int32)
    cross_partner = place_ends(jax.random.randint(seeds[12], (NBLK, NINT), 0, BLK_DEV * FBS), jax.random.fold_in(seeds[12], 1), 0, (BLK_DEV * FBS) - 1).astype(jnp.int32)
    cross_trans = jnp.clip(jnp.exp(math.log(5.0) - 2.3025851 * jax.random.uniform(seeds[13], (NBLK, NINT), jnp.float32) ** block_scale(seeds[13], (NBLK, NINT), ((0, 128),), -0.2, 0.2)), 0.5, 5.0)
    return dict(rhs_matrix=rhs_matrix, trans_x=trans_x, trans_y=trans_y, leak_matrix=leak_matrix, rhs_fracture=rhs_fracture, trans_frac=trans_frac, store_frac=store_frac, mortar_coef=mortar_coef, block_home=block_home, block_len=block_len, mortar_cell=mortar_cell, cross_cell=cross_cell, cross_partner=cross_partner, cross_trans=cross_trans)


def previous_rows(field):
    return jnp.concatenate([jnp.zeros_like(field[:1]), field[:-1]], 0)

def next_rows(field):
    return jnp.concatenate([field[1:], jnp.zeros_like(field[:1])], 0)

def previous_cols(field):
    return jnp.concatenate([jnp.zeros_like(field[:, :1]), field[:, :-1]], 1)

def next_cols(field):
    return jnp.concatenate([field[:, 1:], jnp.zeros_like(field[:, :1])], 1)

def fracture_apply(field, storage, face_trans, face_prev, own_cell, partner_cell, cross_weight):
    result = storage * field + face_trans * (field - next_cols(field)) + face_prev * (field - previous_cols(field))
    flat_field = field.reshape(-1)
    jump_term = cross_weight * (flat_field[own_cell] - flat_field[partner_cell])
    result = result.reshape(-1).at[own_cell].add(jump_term).at[partner_cell].add(-jump_term)
    return result.reshape(field.shape)

def inner_local(former, latter):
    return jnp.sum(former[0] * latter[0]) + jnp.sum(former[1] * latter[1]) + jnp.sum(former[2] * latter[2])

def three_term(image, lanczos_now, lanczos_old, coef_now, coef_old):
    return tuple((part_image - coef_now * part_now - coef_old * part_old for part_image, part_now, part_old in zip(image, lanczos_now, lanczos_old)))

def search_update(precond_now, search_old, search_now, alpha_three, alpha_two, alpha_one):
    return tuple(((part_z - alpha_three * part_old - alpha_two * part_now) / alpha_one for part_z, part_old, part_now in zip(precond_now, search_old, search_now)))

def reference(rhs_matrix, trans_x, trans_y, leak_matrix, rhs_fracture, trans_frac, store_frac, mortar_coef, block_home, block_len, mortar_cell, cross_cell, cross_partner, cross_trans):
    positions = lax.broadcasted_iota(jnp.int32, rhs_fracture.shape, 1)
    cell_mask = (positions < block_len[:, None]).astype(jnp.float32)
    face_trans = trans_frac * cell_mask * next_cols(cell_mask)
    face_prev = previous_cols(face_trans)
    storage = store_frac * cell_mask
    blocks = lax.broadcasted_iota(jnp.int32, cross_cell.shape, 0)
    own_cell = blocks * FBS + cross_cell
    partner_cell = blocks // BLK_DEV * (BLK_DEV * FBS) + cross_partner
    flat_mask = cell_mask.reshape(-1)
    cross_weight = cross_trans * flat_mask[own_cell] * flat_mask[partner_cell]
    home_tile = block_home[:, 0]
    segment = mortar_cell[:, 0]
    grid_rows = (home_tile // N_GY * CX + segment // (CY // FBS))[:, None]
    grid_cols = (home_tile % N_GY * CY + segment % (CY // FBS) * FBS)[:, None] + positions
    target = (grid_rows * NY + grid_cols).astype(jnp.int32)
    tx_prev = previous_rows(trans_x)
    ty_prev = previous_cols(trans_y)
    diag_matrix = leak_matrix + trans_x + tx_prev + trans_y + ty_prev
    diag_frac = (storage + face_trans + face_prev).reshape(-1).at[own_cell].add(cross_weight)
    diag_frac = diag_frac.at[partner_cell].add(cross_weight).reshape(cell_mask.shape)
    safe_frac = diag_frac + 1.0 - cell_mask
    inverse = (1.0 / diag_matrix, cell_mask / safe_frac, cell_mask / (1.0 / mortar_coef + 1.0 / safe_frac))

    def operate(vector):
        field_m, field_f, flux = vector
        out_m = leak_matrix * field_m + trans_x * (field_m - next_rows(field_m)) + tx_prev * (field_m - previous_rows(field_m)) + trans_y * (field_m - next_cols(field_m)) + ty_prev * (field_m - previous_cols(field_m))
        out_m = out_m.reshape(-1).at[target].add(flux).reshape(field_m.shape)
        out_f = fracture_apply(field_f, storage, face_trans, face_prev, own_cell, partner_cell, cross_weight) - flux
        out_l = cell_mask * (field_m.reshape(-1)[target] - field_f - flux / mortar_coef)
        return (out_m, out_f, out_l)

    def precondition(vector):
        return tuple((part_inv * part_vec for part_inv, part_vec in zip(inverse, vector)))
    zero_vec = (jnp.zeros_like(rhs_matrix), jnp.zeros_like(rhs_fracture), jnp.zeros_like(rhs_fracture))
    lanczos_now = (rhs_matrix, rhs_fracture * cell_mask, jnp.zeros_like(rhs_fracture))
    lanczos_old = zero_vec
    precond_now = precondition(lanczos_now)
    gamma_now = jnp.sqrt(inner_local(precond_now, lanczos_now))
    gamma_old = jnp.float32(1.0)
    rhs_scale = gamma_now
    cos_old = jnp.float32(1.0)
    cos_now = jnp.float32(1.0)
    sin_old = jnp.float32(0.0)
    sin_now = jnp.float32(0.0)
    search_old = zero_vec
    search_now = zero_vec
    iterate = zero_vec
    for step in range(ITERS):
        precond_now = tuple((part_z / gamma_now for part_z in precond_now))
        image = operate(precond_now)
        curvature = inner_local(image, precond_now)
        lanczos_new = three_term(image, lanczos_now, lanczos_old, curvature / gamma_now, gamma_now / gamma_old)
        precond_new = precondition(lanczos_new)
        gamma_new = jnp.sqrt(inner_local(precond_new, lanczos_new))
        alpha_zero = cos_now * curvature - cos_old * sin_now * gamma_now
        alpha_one = jnp.sqrt(alpha_zero * alpha_zero + gamma_new * gamma_new)
        alpha_two = sin_now * curvature + cos_old * cos_now * gamma_now
        alpha_three = sin_old * gamma_now
        cos_new = alpha_zero / alpha_one
        sin_new = gamma_new / alpha_one
        search_new = search_update(precond_now, search_old, search_now, alpha_three, alpha_two, alpha_one)
        iterate = tuple((part_x + cos_new * rhs_scale * part_w for part_x, part_w in zip(iterate, search_new)))
        rhs_scale = -sin_new * rhs_scale
        lanczos_old, lanczos_now = (lanczos_now, lanczos_new)
        precond_now = precond_new
        gamma_old, gamma_now = (gamma_now, gamma_new)
        cos_old, cos_now = (cos_now, cos_new)
        sin_old, sin_now = (sin_now, sin_new)
        search_old, search_now = (search_now, search_new)
    return (iterate[0], iterate[1], iterate[2])
```

```python
import jax
import jax.numpy as jnp
from jax import lax
from jax.experimental import pallas as pl
from jax.experimental.pallas import tpu as pltpu
from jax.sharding import PartitionSpec as P

LOGICAL = pl.DeviceIdType.LOGICAL
F32 = jnp.float32
BF16 = jnp.bfloat16

N = 128
ROWS = 256
BAND = 64
ROWS0 = 9
ROWS1 = 6

HOPS = (0, 1, 2, 1)
OFFSETS = sorted(
    (
        (dy, dc, dz, dx)
        for dy in range(4)
        for dc in range(2)
        for dz in range(4)
        for dx in range(4)
        if (dy, dc, dz, dx) != (0, 0, 0, 0)
    ),
    key=lambda o: (-(2 * (HOPS[o[0]] + HOPS[o[2]] + HOPS[o[3]]) + o[1]), o),
)


def split(value):
    high = value.astype(BF16)
    rest = value - high.astype(F32)
    middle = rest.astype(BF16)
    low = (rest - middle.astype(F32)).astype(BF16)
    return [high, middle, low]


def pick(hot, fields):
    parts = [part for field in fields for part in split(field)]
    out = jnp.dot(hot, jnp.concatenate(parts, axis=1), preferred_element_type=F32)
    n = fields[0].shape[1]
    return [
        out[:, 3 * n * i : 3 * n * i + n]
        + out[:, 3 * n * i + n : 3 * n * i + 2 * n]
        + out[:, 3 * n * i + 2 * n : 3 * n * i + 3 * n]
        for i in range(len(fields))
    ]


def fold(value):
    total = value[0:8]
    for i in range(8, value.shape[0], 8):
        total = total + value[i : i + 8]
    return total


def kernel(
    rhs_m_hbm,
    tx_hbm,
    ty_hbm,
    leak_hbm,
    rhs_f_hbm,
    tf_hbm,
    sf_hbm,
    coef_hbm,
    home_hbm,
    len_hbm,
    mcell_hbm,
    cc_hbm,
    cp_hbm,
    ct_hbm,
    out_m,
    out_f,
    out_l,
    rhs_m,
    tx,
    ty,
    leak,
    rhs_f,
    tf,
    sf,
    coef,
    home,
    blen,
    mcell,
    cc,
    cp,
    ct,
    pm,
    co,
    fm,
    send0,
    recv0,
    send1,
    recv1,
    send2,
    recv2,
    hsend_r,
    hrecv_r,
    hsend_c,
    hrecv_c,
    in_sem,
    ssem,
    rsem,
    hs_sem,
    hr_sem,
):
    gx = lax.axis_index("gx")
    gy = lax.axis_index("gy")
    me = gx * 16 + gy

    pairs = [
        (len_hbm, blen),
        (home_hbm, home),
        (mcell_hbm, mcell),
        (cc_hbm, cc),
        (cp_hbm, cp),
        (ct_hbm, ct),
        (tf_hbm, tf),
        (sf_hbm, sf),
        (rhs_f_hbm, rhs_f),
        (coef_hbm, coef),
        (tx_hbm, tx),
        (ty_hbm, ty),
        (leak_hbm, leak),
        (rhs_m_hbm, rhs_m),
    ]
    loads = [pltpu.make_async_copy(a, b, in_sem.at[i]) for i, (a, b) in enumerate(pairs)]
    for load in loads:
        load.start()

    ys = [lax.rem(gx // 2 + d, 4) * 32 for d in range(4)]
    cs = [lax.rem(gx + d, 2) * 16 for d in range(2)]
    zs = [lax.rem(gy // 4 + d, 4) * 4 for d in range(4)]
    xs = [lax.rem(gy + d, 4) for d in range(4)]

    def target(o):
        return (ys[o[0]] + cs[o[1]]) + (zs[o[2]] + xs[o[3]])

    barrier = pltpu.get_barrier_semaphore()
    for o in OFFSETS:
        pl.semaphore_signal(barrier, inc=1, device_id=target(o), device_id_type=LOGICAL)

    below = lax.rem(gx + 1, 8) * 16 + gy
    above = lax.rem(gx + 7, 8) * 16 + gy
    right = gx * 16 + lax.rem(gy + 1, 16)
    left = gx * 16 + lax.rem(gy + 15, 16)
    has_above = jnp.where(gx > 0, 1.0, 0.0).astype(F32)
    has_below = jnp.where(gx < 7, 1.0, 0.0).astype(F32)
    has_left = jnp.where(gy > 0, 1.0, 0.0).astype(F32)
    has_right = jnp.where(gy < 15, 1.0, 0.0).astype(F32)

    lane = lax.broadcasted_iota(jnp.int32, (N, N), 1)
    row = lax.broadcasted_iota(jnp.int32, (N, N), 0)

    for load in loads[:6]:
        load.wait()
    lanef = lane.astype(F32)
    len_row = blen[...].astype(F32)
    cp_row = cp[...]
    pb_row = cp_row // N
    pc_row = cp_row - pb_row * N
    table = jnp.concatenate(
        [
            len_row,
            cc[...].astype(F32),
            pb_row.astype(F32),
            pc_row.astype(F32),
            ct[...],
            jnp.zeros((N - 9, N), F32),
        ],
        axis=0,
    ).T
    len_col = table[:, 0:1]
    own_hot = [lanef == table[:, 1 + k : 2 + k] for k in range(2)]
    part_rows = [lanef == table[:, 3 + k : 4 + k] for k in range(2)]
    part_hot = [lanef == table[:, 5 + k : 6 + k] for k in range(2)]
    weight = []
    for k in range(2):
        part_len = jnp.sum(jnp.where(part_rows[k], len_row, 0.0), axis=1, keepdims=True)
        live = (table[:, 1 + k : 2 + k] < len_col) & (table[:, 5 + k : 6 + k] < part_len)
        weight.append(jnp.where(live, table[:, 7 + k : 8 + k], 0.0))
    gather_hot = jnp.concatenate([jnp.where(h, 1.0, 0.0) for h in part_rows], axis=0).astype(BF16)
    spread_hot = jnp.concatenate(
        [jnp.where(row == pb_row[k : k + 1], 1.0, 0.0) for k in range(2)], axis=1
    ).astype(BF16)

    def spread(own_values, part_values):
        pieces = jnp.concatenate(
            [jnp.where(part_hot[k], part_values[k], 0.0) for k in range(2)], axis=0
        )
        out = pick(spread_hot, [pieces])[0]
        for k in range(2):
            out = out + jnp.where(own_hot[k], own_values[k], 0.0)
        return out

    for load in loads[6:10]:
        load.wait()
    mask = jnp.where(lanef < len_col, 1.0, 0.0)
    face = jnp.where(lanef + 1.0 < len_col, tf[...], 0.0)
    face_prev = pltpu.roll(face, 1, 1)
    diag_f = sf[...] * mask + face + face_prev + spread(weight, weight)
    safe = diag_f + 1.0 - mask
    inv_f = mask / safe
    metric_l = 1.0 / coef[...] + 1.0 / safe
    inv_l = mask / metric_l
    ratio_l = inv_l / coef[...]
    q0 = inv_f * rhs_f[...]

    def off_f(q):
        rows = pick(gather_hot, [q])[0]
        part = [
            jnp.sum(jnp.where(part_hot[k], rows[k * N : k * N + N], 0.0), axis=1, keepdims=True)
            for k in range(2)
        ]
        own = [jnp.sum(jnp.where(own_hot[k], q, 0.0), axis=1, keepdims=True) for k in range(2)]
        crossing = spread(
            [weight[k] * part[k] for k in range(2)], [weight[k] * own[k] for k in range(2)]
        )
        return face * pltpu.roll(q, N - 1, 1) + face_prev * pltpu.roll(q, 1, 1) + crossing

    q1 = -inv_f * off_f(q0)

    home_hit = row == home[...]
    first = jnp.min(jnp.where(home_hit, lanef, 1e3), axis=1, keepdims=True)
    last = jnp.max(jnp.where(home_hit, lanef, -1.0), axis=1, keepdims=True)
    slots = [
        jnp.where(lanef == first, 1.0, 0.0),
        jnp.where((lanef == last) & (last > first), 1.0, 0.0),
    ]
    mcell_row = mcell[...].astype(F32)
    cells = [jnp.sum(s * mcell_row, axis=1, keepdims=True) for s in slots]
    slot_hot = jnp.concatenate(slots, axis=0).astype(BF16)
    packed = pick(slot_hot, [inv_l, ratio_l, q0, q1])
    for i, value in enumerate(packed):
        send0[:, 2 * i, :] = value[:N]
        send0[:, 2 * i + 1, :] = value[N:]
    send0[:, 8, :] = jnp.where(lane < BAND, cells[0], cells[1])
    recv0[pl.ds(me, 1)] = send0[pl.ds(me, 1)]

    fm[0] = q0
    fm[1] = q1

    for load in loads[10:]:
        load.wait()
    sub8 = lax.broadcasted_iota(jnp.int32, (8, N), 0)
    lane8 = lax.broadcasted_iota(jnp.int32, (8, N), 1)
    ends = jnp.where(
        ((sub8 == 0) & (lane8 == 0)) | ((sub8 == 1) & (lane8 == N - 1)), 1.0, 0.0
    ).astype(BF16)

    def end_cols(field):
        parts = jnp.concatenate(split(field), axis=0)
        out = lax.dot_general(
            ends, parts, (((1,), (1,)), ((), ())), preferred_element_type=F32
        )
        return out[:, :ROWS] + out[:, ROWS : 2 * ROWS] + out[:, 2 * ROWS :]

    def halo_copy(phase, way):
        device = (below, above, right, left)[way]
        send, recv = (hsend_r, hrecv_r) if way < 2 else (hsend_c, hrecv_c)
        return pltpu.make_async_remote_copy(
            send.at[phase, way % 2],
            recv.at[phase, way % 2],
            hs_sem.at[phase, way],
            hr_sem.at[phase, way],
            device_id=device,
            device_id_type=LOGICAL,
        )

    def halo_send(phase, field):
        hsend_r[phase, 0] = field[ROWS - 1 : ROWS]
        hsend_r[phase, 1] = field[0:1]
        cols = end_cols(field)
        hsend_c[phase, 0] = cols[1:2]
        hsend_c[phase, 1] = cols[0:1]
        for way in range(4):
            halo_copy(phase, way).start()

    def wide_cols(before, after):
        both = jnp.concatenate([before, after, jnp.zeros((6, ROWS), F32)], axis=0)
        cols = both.T
        return cols[:, 0:1], cols[:, 1:2]

    row_m = lax.broadcasted_iota(jnp.int32, (ROWS, N), 0)
    lane_m = lax.broadcasted_iota(jnp.int32, (ROWS, N), 1)

    def off_m(p, phase):
        for way in range(4):
            halo_copy(phase, way).wait_recv()
        top = hrecv_r[phase, 0] * has_above
        bottom = hrecv_r[phase, 1] * has_below
        before, after = wide_cols(hrecv_c[phase, 0] * has_left, hrecv_c[phase, 1] * has_right)
        up = jnp.where(row_m == 0, top, pltpu.roll(p, 1, 0))
        down = jnp.where(row_m == ROWS - 1, bottom, pltpu.roll(p, ROWS - 1, 0))
        lft = jnp.where(lane_m == 0, before, pltpu.roll(p, 1, 1))
        rgt = jnp.where(lane_m == N - 1, after, pltpu.roll(p, N - 1, 1))
        return co[0] * down + co[1] * up + co[2] * rgt + co[3] * lft

    hsend_r[0, 0] = tx[ROWS - 1 : ROWS, :]
    hsend_c[0, 0] = end_cols(ty[...])[1:2]

    pl.semaphore_wait(barrier, N - 1)
    halo_copy(0, 0).start()
    halo_copy(0, 2).start()

    def send_to_home(o):
        t = target(o)
        pltpu.make_async_remote_copy(
            send0.at[t],
            recv0.at[me],
            ssem.at[0],
            rsem.at[0],
            device_id=t,
            device_id_type=LOGICAL,
        ).start()

    for o in OFFSETS[:40]:
        send_to_home(o)

    halo_copy(0, 0).wait_recv()
    halo_copy(0, 2).wait_recv()
    tx_prev = jnp.where(row_m == 0, hrecv_r[0, 0] * has_above, pltpu.roll(tx[...], 1, 0))
    left_col, _ = wide_cols(hrecv_c[0, 0] * has_left, jnp.zeros((1, ROWS), F32))
    ty_prev = jnp.where(lane_m == 0, left_col, pltpu.roll(ty[...], 1, 1))
    diag_m = leak[...] + tx[...] + tx_prev + ty[...] + ty_prev
    inv_m = 1.0 / diag_m
    p0 = rhs_m[...] * inv_m
    halo_send(1, p0)
    pm[0] = p0
    co[0] = tx[...] * inv_m
    co[1] = tx_prev * inv_m
    co[2] = ty[...] * inv_m
    co[3] = ty_prev * inv_m
    co[4] = diag_m
    co[5] = inv_m

    for o in OFFSETS[40:80]:
        send_to_home(o)

    p1 = -off_m(pm[0], 1)
    halo_send(2, p1)
    pm[1] = p1

    for o in OFFSETS[80:]:
        send_to_home(o)

    slot_hot_t = jnp.concatenate([s.T for s in slots], axis=1).astype(BF16)
    q2_part = -inv_f * off_f(fm[1])
    pm[2] = -off_m(pm[1], 2)
    dm = co[4]
    moments = [
        fold(dm * pm[0] * pm[0]) + fold(safe * fm[0] * fm[0]),
        fold(dm * pm[0] * pm[1]) + fold(safe * fm[0] * fm[1]),
        fold(dm * pm[1] * pm[1]) + fold(safe * fm[1] * fm[1]),
    ]

    def all_arrived(send, recv, i):
        return pltpu.make_async_remote_copy(
            send.at[pl.ds(0, N - 1)],
            recv.at[pl.ds(0, N - 1)],
            ssem.at[i],
            rsem.at[i],
            device_id=right,
            device_id_type=LOGICAL,
        )

    all_arrived(send0, recv0, 0).wait_recv()
    lane_band = jnp.where(lane < BAND, lane, lane - BAND).astype(F32)
    hit = jnp.where(recv0[:, 8, :] == lane_band, 1.0, 0.0)
    hit_slots = jnp.concatenate(
        [jnp.where(lane < BAND, hit, 0.0), jnp.where(lane < BAND, 0.0, hit)], axis=0
    ).astype(BF16)
    hit_t = hit.T
    hit_rows = jnp.concatenate([hit_t[:BAND], hit_t[BAND:]], axis=1).astype(BF16)

    def sample(fields):
        return pick(hit_slots, [jnp.concatenate([f, f], axis=0) for f in fields])

    p0_at, p1_at = sample([pm[0, 0:BAND], pm[1, 0:BAND]])

    def both(r):
        return jnp.concatenate([recv0[:, r, :], recv0[:, r + 1, :]], axis=0)

    inv_at, ratio_at = both(0), both(2)
    l1 = inv_at * (p0_at - both(4))
    l2 = inv_at * (p1_at - both(6)) - (ratio_at + 1.0) * l1
    pm[2, 0:BAND] += co[5, 0:BAND] * pick(hit_rows, [l1])[0]
    p2 = pm[2]
    halo_send(3, p2)
    p2_at = sample([p2[0:BAND]])[0]
    for i, value in enumerate((l1, l2, p2_at)):
        send1[:, 2 * i, :] = value[:N]
        send1[:, 2 * i + 1, :] = value[N:]
    recv1[pl.ds(me, 1)] = send1[pl.ds(me, 1)]
    for o in OFFSETS:
        t = target(o)
        pltpu.make_async_remote_copy(
            send1.at[t],
            recv1.at[me],
            ssem.at[1],
            rsem.at[1],
            device_id=t,
            device_id_type=LOGICAL,
        ).start()
    pm[3] = -off_m(pm[2], 3)
    pm[3, 0:BAND] += co[5, 0:BAND] * pick(hit_rows, [l2])[0]
    d2 = co[4] * pm[2]
    moments.append(fold(d2 * pm[1]))
    moments.append(fold(d2 * pm[2]))
    moments.append(fold(d2 * pm[3]))
    moments.append(fold(co[4] * pm[3] * pm[3]))

    all_arrived(send1, recv1, 1).wait_recv()

    def returned(r):
        return jnp.concatenate([recv1[:, r, :], recv1[:, r + 1, :]], axis=0)

    l1, l2, p2_at = pick(slot_hot_t, [returned(0), returned(2), returned(4)])
    q2 = q2_part - inv_f * l1
    q3 = -inv_f * (off_f(q2) + l2)
    l3 = inv_l * (p2_at - q2) - (ratio_l + 1.0) * l2
    fm[2] = q2
    fm[3] = l1
    fm[4] = l2
    m1, m2 = metric_l * l1, metric_l * l2
    s2 = safe * q2
    moments[2] += fold(m1 * l1)
    moments[3] += fold(s2 * fm[1] + m1 * l2)
    moments[4] += fold(s2 * q2 + m2 * l2)
    moments[5] += fold(s2 * q3 + m2 * l3)
    moments[6] += fold(safe * q3 * q3 + metric_l * l3 * l3)
    rows = [jnp.sum(m, axis=0, keepdims=True) for m in moments]
    sums = jnp.sum(jnp.concatenate(rows + [jnp.zeros((1, N), F32)], axis=0), axis=1, keepdims=True)
    mine = jnp.sum(jnp.where(lane8 == sub8, sums, 0.0), axis=0, keepdims=True)
    send2[...] = mine
    recv2[pl.ds(me, 1)] = mine[None]
    for o in OFFSETS:
        pltpu.make_async_remote_copy(
            send2,
            recv2.at[me],
            ssem.at[2],
            rsem.at[2],
            device_id=target(o),
            device_id_type=LOGICAL,
        ).start()
    all_arrived(recv2, recv2, 2).wait_recv()
    total = jnp.sum(recv2[...], axis=0)
    mu = [jnp.broadcast_to(total[:, i : i + 1], (1, N)) for i in range(7)]

    n0 = mu[0]
    a0 = mu[1] / n0
    n1 = mu[2] - a0 * mu[1]
    a1 = (mu[3] - a0 * (mu[2] + n1)) / n1
    b1 = n1 / n0
    c1 = -(a0 + a1)
    c0 = a0 * a1 - b1
    n2 = mu[4] + c1 * mu[3] + c0 * mu[2]
    a2 = (mu[5] + c1 * mu[4] + c0 * mu[3]) / n2 + c1
    b2 = n2 / n1
    square = mu[6] + 2.0 * c1 * mu[5] + (c1 * c1 + 2.0 * c0) * mu[4] + 2.0 * c0 * c1 * mu[3] + c0 * c0 * mu[2]
    n3 = square - (a2 * a2 + b2) * n2
    gammas = [jnp.sqrt(n0), jnp.sqrt(b1), jnp.sqrt(b2), jnp.sqrt(n3 / n2)]
    curvatures = [a0 + 1.0, a1 + 1.0, a2 + 1.0]
    i0, i1, i2 = lax.rsqrt(n0), lax.rsqrt(n1), lax.rsqrt(n2)
    zero = jnp.zeros_like(n0)
    one = jnp.ones_like(n0)
    basis = [(i0, zero, zero), (-a0 * i1, i1, zero), (c0 * i2, c1 * i2, i2)]
    cos_old, cos_now, sin_old, sin_now = one, one, zero, zero
    rhs_scale = gammas[0]
    search_old = search_now = iterate = (zero, zero, zero)
    for k in range(3):
        gamma, gamma_new = gammas[k], gammas[k + 1]
        alpha_zero = cos_now * curvatures[k] - cos_old * sin_now * gamma
        alpha_one = jnp.sqrt(alpha_zero * alpha_zero + gamma_new * gamma_new)
        alpha_two = sin_now * curvatures[k] + cos_old * cos_now * gamma
        alpha_three = sin_old * gamma
        cos_new, sin_new = alpha_zero / alpha_one, gamma_new / alpha_one
        search_new = tuple(
            (z - alpha_three * old - alpha_two * now) / alpha_one
            for z, old, now in zip(basis[k], search_old, search_now)
        )
        iterate = tuple(x + cos_new * rhs_scale * w for x, w in zip(iterate, search_new))
        rhs_scale = -sin_new * rhs_scale
        cos_old, cos_now, sin_old, sin_now = cos_now, cos_new, sin_now, sin_new
        search_old, search_now = search_now, search_new
    x0, x1, x2 = iterate
    out_m[...] = x0 * pm[0] + x1 * pm[1] + x2 * pm[2]
    out_f[...] = x0 * fm[0] + x1 * fm[1] + x2 * fm[2]
    out_l[...] = x1 * fm[3] + x2 * fm[4]

    all_arrived(send0, recv0, 0).wait_send()
    all_arrived(send1, recv1, 1).wait_send()
    all_arrived(recv2, recv2, 2).wait_send()
    halo_copy(0, 0).wait_send()
    halo_copy(0, 2).wait_send()
    for phase in range(1, 4):
        for way in range(4):
            halo_copy(phase, way).wait_send()


def local(
    rhs_matrix,
    trans_x,
    trans_y,
    leak_matrix,
    rhs_fracture,
    trans_frac,
    store_frac,
    mortar_coef,
    block_home,
    block_len,
    mortar_cell,
    cross_cell,
    cross_partner,
    cross_trans,
):
    tile, block = (ROWS, N), (N, N)
    vmem = lambda shape, kind=F32: pltpu.VMEM(shape, kind)
    return pl.pallas_call(
        kernel,
        out_shape=(
            jax.ShapeDtypeStruct(tile, F32),
            jax.ShapeDtypeStruct(block, F32),
            jax.ShapeDtypeStruct(block, F32),
        ),
        in_specs=[pl.BlockSpec(memory_space=pl.ANY)] * 14,
        out_specs=(pl.BlockSpec(memory_space=pltpu.VMEM),) * 3,
        scratch_shapes=[vmem(tile)] * 4
        + [vmem(block)] * 4
        + [vmem((1, N), jnp.int32)] * 3
        + [vmem((2, N), jnp.int32)] * 2
        + [vmem((2, N))]
        + [
            vmem((4,) + tile),
            vmem((6,) + tile),
            vmem((5,) + block),
            vmem((N, ROWS0, N)),
            vmem((N, ROWS0, N)),
            vmem((N, ROWS1, N)),
            vmem((N, ROWS1, N)),
            vmem((1, N)),
            vmem((N, 1, N)),
            vmem((4, 2, 1, N)),
            vmem((4, 2, 1, N)),
            vmem((4, 2, 1, ROWS)),
            vmem((4, 2, 1, ROWS)),
            pltpu.SemaphoreType.DMA((14,)),
            pltpu.SemaphoreType.DMA((3,)),
            pltpu.SemaphoreType.DMA((3,)),
            pltpu.SemaphoreType.DMA((4, 4)),
            pltpu.SemaphoreType.DMA((4, 4)),
        ],
        compiler_params=pltpu.CompilerParams(
            collective_id=0, has_side_effects=True, vmem_limit_bytes=40 * 2**20
        ),
    )(
        rhs_matrix,
        trans_x,
        trans_y,
        leak_matrix,
        rhs_fracture,
        trans_frac,
        store_frac,
        mortar_coef,
        block_home.T,
        block_len.reshape(1, N),
        mortar_cell.T,
        cross_cell.T,
        cross_partner.T,
        cross_trans.T,
    )


def solution(mesh):
    tiles, blocks = P("gx", "gy"), P(("gx", "gy"), None)
    return jax.shard_map(
        local,
        mesh=mesh,
        in_specs=(tiles,) * 4 + (blocks,) * 5 + (P(("gx", "gy")),) + (blocks,) * 4,
        out_specs=(tiles, blocks, blocks),
        check_vma=False,
    )
```

```python
import jax
import jax.numpy as jnp
from jax import lax
from jax.experimental import pallas as pl
from jax.experimental.pallas import tpu as pltpu
from jax.sharding import PartitionSpec as P

LOGICAL = pl.DeviceIdType.LOGICAL
F32 = jnp.float32
BF16 = jnp.bfloat16

N = 128
ROWS = 256
BAND = 64
ROWS0 = 9
ROWS1 = 6

FIRST = 100

HOPS = (0, 1, 2, 1)
OFFSETS = sorted(
    (
        (dy, dc, dz, dx)
        for dy in range(4)
        for dc in range(2)
        for dz in range(4)
        for dx in range(4)
        if (dy, dc, dz, dx) != (0, 0, 0, 0)
    ),
    key=lambda o: (-(2 * (HOPS[o[0]] + HOPS[o[2]] + HOPS[o[3]]) + o[1]), o),
)


def split(value):
    high = value.astype(BF16)
    rest = value - high.astype(F32)
    middle = rest.astype(BF16)
    low = (rest - middle.astype(F32)).astype(BF16)
    return [high, middle, low]


def pick(hot, fields):
    parts = [part for field in fields for part in split(field)]
    out = jnp.dot(hot, jnp.concatenate(parts, axis=1), preferred_element_type=F32)
    n = fields[0].shape[1]
    return [
        out[:, 3 * n * i : 3 * n * i + n]
        + out[:, 3 * n * i + n : 3 * n * i + 2 * n]
        + out[:, 3 * n * i + 2 * n : 3 * n * i + 3 * n]
        for i in range(len(fields))
    ]


def fold(value):
    total = value[0:8]
    for i in range(8, value.shape[0], 8):
        total = total + value[i : i + 8]
    return total


def kernel(
    rhs_m_hbm,
    tx_hbm,
    ty_hbm,
    leak_hbm,
    rhs_f_hbm,
    tf_hbm,
    sf_hbm,
    coef_hbm,
    home_hbm,
    len_hbm,
    mcell_hbm,
    cc_hbm,
    cp_hbm,
    ct_hbm,
    pm,
    fm,
    factors,
    rhs_m,
    tx,
    ty,
    leak,
    rhs_f,
    tf,
    sf,
    coef,
    home,
    blen,
    mcell,
    cc,
    cp,
    ct,
    p3_ref,
    co,
    send0,
    recv0,
    send1,
    recv1,
    send2,
    recv2,
    hsend_r,
    hrecv_r,
    hsend_c,
    hrecv_c,
    esend_r,
    erecv_r,
    esend_c,
    erecv_c,
    in_sem,
    ssem,
    rsem,
    hs_sem,
    hr_sem,
    es_sem,
    er_sem,
):
    gx = lax.axis_index("gx")
    gy = lax.axis_index("gy")
    me = gx * 16 + gy

    pairs = [
        (len_hbm, blen),
        (home_hbm, home),
        (mcell_hbm, mcell),
        (cc_hbm, cc),
        (cp_hbm, cp),
        (ct_hbm, ct),
        (tf_hbm, tf),
        (sf_hbm, sf),
        (rhs_f_hbm, rhs_f),
        (coef_hbm, coef),
        (tx_hbm, tx),
        (ty_hbm, ty),
        (leak_hbm, leak),
        (rhs_m_hbm, rhs_m),
    ]
    loads = [pltpu.make_async_copy(a, b, in_sem.at[i]) for i, (a, b) in enumerate(pairs)]
    for load in loads:
        load.start()

    ys = [lax.rem(gx // 2 + d, 4) * 32 for d in range(4)]
    cs = [lax.rem(gx + d, 2) * 16 for d in range(2)]
    zs = [lax.rem(gy // 4 + d, 4) * 4 for d in range(4)]
    xs = [lax.rem(gy + d, 4) for d in range(4)]

    def target(o):
        return (ys[o[0]] + cs[o[1]]) + (zs[o[2]] + xs[o[3]])

    barrier = pltpu.get_barrier_semaphore()
    for o in OFFSETS:
        pl.semaphore_signal(barrier, inc=1, device_id=target(o), device_id_type=LOGICAL)

    below = lax.rem(gx + 1, 8) * 16 + gy
    above = lax.rem(gx + 7, 8) * 16 + gy
    right = gx * 16 + lax.rem(gy + 1, 16)
    left = gx * 16 + lax.rem(gy + 15, 16)
    below_right = lax.rem(gx + 1, 8) * 16 + lax.rem(gy + 1, 16)
    above_right = lax.rem(gx + 7, 8) * 16 + lax.rem(gy + 1, 16)
    below_left = lax.rem(gx + 1, 8) * 16 + lax.rem(gy + 15, 16)
    has_above = jnp.where(gx > 0, 1.0, 0.0).astype(F32)
    has_below = jnp.where(gx < 7, 1.0, 0.0).astype(F32)
    has_left = jnp.where(gy > 0, 1.0, 0.0).astype(F32)
    has_right = jnp.where(gy < 15, 1.0, 0.0).astype(F32)

    lane = lax.broadcasted_iota(jnp.int32, (N, N), 1)
    row = lax.broadcasted_iota(jnp.int32, (N, N), 0)

    for load in loads[:6]:
        load.wait()
    lanef = lane.astype(F32)
    len_row = blen[...].astype(F32)
    cp_row = cp[...]
    pb_row = cp_row // N
    pc_row = cp_row - pb_row * N
    table = jnp.concatenate(
        [
            len_row,
            cc[...].astype(F32),
            pb_row.astype(F32),
            pc_row.astype(F32),
            ct[...],
            jnp.zeros((N - 9, N), F32),
        ],
        axis=0,
    ).T
    len_col = table[:, 0:1]
    own_hot = [lanef == table[:, 1 + k : 2 + k] for k in range(2)]
    part_rows = [lanef == table[:, 3 + k : 4 + k] for k in range(2)]
    part_hot = [lanef == table[:, 5 + k : 6 + k] for k in range(2)]
    weight = []
    for k in range(2):
        part_len = jnp.sum(jnp.where(part_rows[k], len_row, 0.0), axis=1, keepdims=True)
        live = (table[:, 1 + k : 2 + k] < len_col) & (table[:, 5 + k : 6 + k] < part_len)
        weight.append(jnp.where(live, table[:, 7 + k : 8 + k], 0.0))
    gather_hot = jnp.concatenate([jnp.where(h, 1.0, 0.0) for h in part_rows], axis=0).astype(BF16)
    spread_hot = jnp.concatenate(
        [jnp.where(row == pb_row[k : k + 1], 1.0, 0.0) for k in range(2)], axis=1
    ).astype(BF16)

    def spread(own_values, part_values):
        pieces = jnp.concatenate(
            [jnp.where(part_hot[k], part_values[k], 0.0) for k in range(2)], axis=0
        )
        out = pick(spread_hot, [pieces])[0]
        for k in range(2):
            out = out + jnp.where(own_hot[k], own_values[k], 0.0)
        return out

    for load in loads[6:10]:
        load.wait()
    mask = jnp.where(lanef < len_col, 1.0, 0.0)
    face = jnp.where(lanef + 1.0 < len_col, tf[...], 0.0)
    face_prev = pltpu.roll(face, 1, 1)
    diag_f = sf[...] * mask + face + face_prev + spread(weight, weight)
    safe = diag_f + 1.0 - mask
    inv_f = mask / safe
    metric_l = 1.0 / coef[...] + 1.0 / safe
    inv_l = mask / metric_l
    ratio_l = inv_l / coef[...]
    q0 = inv_f * rhs_f[...]

    def off_f(q):
        rows = pick(gather_hot, [q])[0]
        part = [
            jnp.sum(jnp.where(part_hot[k], rows[k * N : k * N + N], 0.0), axis=1, keepdims=True)
            for k in range(2)
        ]
        own = [jnp.sum(jnp.where(own_hot[k], q, 0.0), axis=1, keepdims=True) for k in range(2)]
        crossing = spread(
            [weight[k] * part[k] for k in range(2)], [weight[k] * own[k] for k in range(2)]
        )
        return face * pltpu.roll(q, N - 1, 1) + face_prev * pltpu.roll(q, 1, 1) + crossing

    q1 = -inv_f * off_f(q0)

    home_hit = row == home[...]
    first = jnp.min(jnp.where(home_hit, lanef, 1e3), axis=1, keepdims=True)
    last = jnp.max(jnp.where(home_hit, lanef, -1.0), axis=1, keepdims=True)
    slots = [
        jnp.where(lanef == first, 1.0, 0.0),
        jnp.where((lanef == last) & (last > first), 1.0, 0.0),
    ]
    mcell_row = mcell[...].astype(F32)
    cells = [jnp.sum(s * mcell_row, axis=1, keepdims=True) for s in slots]
    slot_hot = jnp.concatenate(slots, axis=0).astype(BF16)
    packed = pick(slot_hot, [inv_l, ratio_l, q0, q1])
    for i, value in enumerate(packed):
        send0[:, 2 * i, :] = value[:N]
        send0[:, 2 * i + 1, :] = value[N:]
    send0[:, 8, :] = jnp.where(lane < BAND, cells[0], cells[1])
    recv0[pl.ds(me, 1)] = send0[pl.ds(me, 1)]

    fm[0] = q0
    fm[1] = q1

    for load in loads[10:]:
        load.wait()
    sub8 = lax.broadcasted_iota(jnp.int32, (8, N), 0)
    lane8 = lax.broadcasted_iota(jnp.int32, (8, N), 1)
    ends = jnp.where(
        ((sub8 == 0) & (lane8 == 0)) | ((sub8 == 1) & (lane8 == N - 1)), 1.0, 0.0
    ).astype(BF16)

    def end_cols(fields):
        parts = jnp.concatenate([part for field in fields for part in split(field)], axis=0)
        out = lax.dot_general(ends, parts, (((1,), (1,)), ((), ())), preferred_element_type=F32)
        pieces = [out[:, ROWS * k : ROWS * (k + 1)] for k in range(3 * len(fields))]
        return [pieces[3 * k] + pieces[3 * k + 1] + pieces[3 * k + 2] for k in range(len(fields))]

    def halo_copy(phase, way):
        device = (below, above, right, left)[way]
        send, recv = (hsend_r, hrecv_r) if way < 2 else (hsend_c, hrecv_c)
        return pltpu.make_async_remote_copy(
            send.at[phase, way % 2],
            recv.at[phase, way % 2],
            hs_sem.at[phase, way],
            hr_sem.at[phase, way],
            device_id=device,
            device_id_type=LOGICAL,
        )

    def halo_send(phase, field):
        hsend_r[phase, 0] = field[ROWS - 1 : ROWS]
        hsend_r[phase, 1] = field[0:1]
        cols = end_cols([field])[0]
        hsend_c[phase, 0] = cols[1:2]
        hsend_c[phase, 1] = cols[0:1]
        for way in range(4):
            halo_copy(phase, way).start()

    def as_cols(rows):
        cols = jnp.concatenate(rows + [jnp.zeros((8 - len(rows), ROWS), F32)], axis=0).T
        return [cols[:, k : k + 1] for k in range(len(rows))]

    row_m = lax.broadcasted_iota(jnp.int32, (ROWS, N), 0)
    lane_m = lax.broadcasted_iota(jnp.int32, (ROWS, N), 1)

    def off_m(p, top, bottom, before, after):
        up = jnp.where(row_m == 0, top, pltpu.roll(p, 1, 0))
        down = jnp.where(row_m == ROWS - 1, bottom, pltpu.roll(p, ROWS - 1, 0))
        lft = jnp.where(lane_m == 0, before, pltpu.roll(p, 1, 1))
        rgt = jnp.where(lane_m == N - 1, after, pltpu.roll(p, N - 1, 1))
        return co[0] * down + co[1] * up + co[2] * rgt + co[3] * lft

    def halo(phase):
        for way in range(4):
            halo_copy(phase, way).wait_recv()
        before, after = as_cols([hrecv_c[phase, 0] * has_left, hrecv_c[phase, 1] * has_right])
        return hrecv_r[phase, 0] * has_above, hrecv_r[phase, 1] * has_below, before, after

    tx_up = jnp.where(row_m == 0, 0.0, pltpu.roll(tx[...], 1, 0))
    ty_left = jnp.where(lane_m == 0, 0.0, pltpu.roll(ty[...], 1, 1))
    partial = leak[...] + tx[...] + tx_up + ty[...] + ty_left
    esend_r[0] = tx[ROWS - 1 : ROWS]
    esend_r[1] = rhs_m[ROWS - 1 : ROWS]
    esend_r[2] = partial[ROWS - 1 : ROWS]
    esend_r[3] = rhs_m[0:1]
    esend_r[4] = partial[0:1]
    esend_r[5] = tx[ROWS - 1 : ROWS]
    esend_r[6] = ty[ROWS - 1 : ROWS]
    esend_r[7] = ty[0:1]
    esend_r[8] = tx[ROWS - 1 : ROWS]
    ty_cols, rhs_cols, partial_cols = end_cols([ty[...], rhs_m[...], partial])
    esend_c[0] = ty_cols[1:2]
    esend_c[1] = rhs_cols[1:2]
    esend_c[2] = partial_cols[1:2]
    esend_c[3] = rhs_cols[0:1]
    esend_c[4] = partial_cols[0:1]

    def edge_copy(i):
        send, recv, start, count, device = (
            (esend_r, erecv_r, 0, 3, below),
            (esend_r, erecv_r, 3, 2, above),
            (esend_r, erecv_r, 5, 2, below_right),
            (esend_r, erecv_r, 7, 1, above_right),
            (esend_r, erecv_r, 8, 1, below_left),
            (esend_c, erecv_c, 0, 3, right),
            (esend_c, erecv_c, 3, 2, left),
        )[i]
        return pltpu.make_async_remote_copy(
            send.at[pl.ds(start, count)],
            recv.at[pl.ds(start, count)],
            es_sem.at[i],
            er_sem.at[i],
            device_id=device,
            device_id_type=LOGICAL,
        )

    pl.semaphore_wait(barrier, N - 1)
    for i in range(7):
        edge_copy(i).start()

    def send_to_home(o):
        t = target(o)
        pltpu.make_async_remote_copy(
            send0.at[t],
            recv0.at[me],
            ssem.at[0],
            rsem.at[0],
            device_id=t,
            device_id_type=LOGICAL,
        ).start()

    for o in OFFSETS[:FIRST]:
        send_to_home(o)

    for i in range(7):
        edge_copy(i).wait_recv()
    lane_1 = lax.broadcasted_iota(jnp.int32, (1, N), 1)

    def corner(value, factor):
        return jnp.where(lane_1 == 0, value, 0.0) * factor

    def corner_col(value, factor):
        return jnp.concatenate([corner(value, factor), jnp.zeros((1, N), F32)], axis=1)

    diag_above = erecv_r[2] + corner(pltpu.roll(erecv_r[6], 1, 1), has_left)
    diag_below = erecv_r[4] + tx[ROWS - 1 : ROWS] + corner(pltpu.roll(erecv_r[7], 1, 1), has_left)
    diag_left = erecv_c[2] + corner_col(pltpu.roll(erecv_r[5], 1, 1), has_above)
    diag_right = erecv_c[4] + esend_c[0] + corner_col(erecv_r[8], has_above)
    p0_above = erecv_r[1] / diag_above * has_above
    p0_below = erecv_r[3] / diag_below * has_below
    ty_col, p0_left, p0_right = as_cols(
        [
            erecv_c[0] * has_left,
            erecv_c[1] / diag_left * has_left,
            erecv_c[3] / diag_right * has_right,
        ]
    )
    tx_prev = jnp.where(row_m == 0, erecv_r[0] * has_above, pltpu.roll(tx[...], 1, 0))
    ty_prev = jnp.where(lane_m == 0, ty_col, pltpu.roll(ty[...], 1, 1))
    diag_m = leak[...] + tx[...] + tx_prev + ty[...] + ty_prev
    inv_m = 1.0 / diag_m
    pm[0] = rhs_m[...] * inv_m
    co[0] = tx[...] * inv_m
    co[1] = tx_prev * inv_m
    co[2] = ty[...] * inv_m
    co[3] = ty_prev * inv_m
    co[4] = diag_m
    co[5] = inv_m
    p1 = -off_m(pm[0], p0_above, p0_below, p0_left, p0_right)
    halo_send(0, p1)
    pm[1] = p1

    for o in OFFSETS[FIRST:]:
        send_to_home(o)

    slot_hot_t = jnp.concatenate([s.T for s in slots], axis=1).astype(BF16)
    q2_part = -inv_f * off_f(fm[1])
    pm[2] = -off_m(pm[1], *halo(0))
    dm = co[4]
    moments = [
        fold(dm * pm[0] * pm[0]) + fold(safe * fm[0] * fm[0]),
        fold(dm * pm[0] * pm[1]) + fold(safe * fm[0] * fm[1]),
        fold(dm * pm[1] * pm[1]) + fold(safe * fm[1] * fm[1]),
    ]

    def all_arrived(send, recv, i):
        return pltpu.make_async_remote_copy(
            send.at[pl.ds(0, N - 1)],
            recv.at[pl.ds(0, N - 1)],
            ssem.at[i],
            rsem.at[i],
            device_id=right,
            device_id_type=LOGICAL,
        )

    all_arrived(send0, recv0, 0).wait_recv()
    lane_band = jnp.where(lane < BAND, lane, lane - BAND).astype(F32)
    hit = jnp.where(recv0[:, 8, :] == lane_band, 1.0, 0.0)
    hit_slots = jnp.concatenate(
        [jnp.where(lane < BAND, hit, 0.0), jnp.where(lane < BAND, 0.0, hit)], axis=0
    ).astype(BF16)
    hit_t = hit.T
    hit_rows = jnp.concatenate([hit_t[:BAND], hit_t[BAND:]], axis=1).astype(BF16)

    def sample(fields):
        return pick(hit_slots, [jnp.concatenate([f, f], axis=0) for f in fields])

    p0_at, p1_at = sample([pm[0, 0:BAND], pm[1, 0:BAND]])

    def both(r):
        return jnp.concatenate([recv0[:, r, :], recv0[:, r + 1, :]], axis=0)

    inv_at, ratio_at = both(0), both(2)
    l1 = inv_at * (p0_at - both(4))
    l2 = inv_at * (p1_at - both(6)) - (ratio_at + 1.0) * l1
    pm[2, 0:BAND] += co[5, 0:BAND] * pick(hit_rows, [l1])[0]
    p2 = pm[2]
    halo_send(1, p2)
    p2_at = sample([p2[0:BAND]])[0]
    for i, value in enumerate((l1, l2, p2_at)):
        send1[:, 2 * i, :] = value[:N]
        send1[:, 2 * i + 1, :] = value[N:]
    recv1[pl.ds(me, 1)] = send1[pl.ds(me, 1)]
    for o in OFFSETS:
        t = target(o)
        pltpu.make_async_remote_copy(
            send1.at[t],
            recv1.at[me],
            ssem.at[1],
            rsem.at[1],
            device_id=t,
            device_id_type=LOGICAL,
        ).start()
    p3_ref[...] = -off_m(pm[2], *halo(1))
    p3_ref[0:BAND] += co[5, 0:BAND] * pick(hit_rows, [l2])[0]
    d2 = co[4] * pm[2]
    moments.append(fold(d2 * pm[1]))
    moments.append(fold(d2 * pm[2]))
    p3 = p3_ref[...]
    moments.append(fold(d2 * p3))
    moments.append(fold(co[4] * p3 * p3))

    all_arrived(send1, recv1, 1).wait_recv()

    def returned(r):
        return jnp.concatenate([recv1[:, r, :], recv1[:, r + 1, :]], axis=0)

    l1, l2, p2_at = pick(slot_hot_t, [returned(0), returned(2), returned(4)])
    q2 = q2_part - inv_f * l1
    q3 = -inv_f * (off_f(q2) + l2)
    l3 = inv_l * (p2_at - q2) - (ratio_l + 1.0) * l2
    fm[2] = q2
    fm[3] = l1
    fm[4] = l2
    m1, m2 = metric_l * l1, metric_l * l2
    s2 = safe * q2
    moments[2] += fold(m1 * l1)
    moments[3] += fold(s2 * fm[1] + m1 * l2)
    moments[4] += fold(s2 * q2 + m2 * l2)
    moments[5] += fold(s2 * q3 + m2 * l3)
    moments[6] += fold(safe * q3 * q3 + metric_l * l3 * l3)
    rows = [jnp.sum(m, axis=0, keepdims=True) for m in moments]
    sums = jnp.sum(jnp.concatenate(rows + [jnp.zeros((1, N), F32)], axis=0), axis=1, keepdims=True)
    mine = jnp.sum(jnp.where(lane8 == sub8, sums, 0.0), axis=0, keepdims=True)
    send2[...] = mine
    recv2[pl.ds(me, 1)] = mine[None]
    for o in OFFSETS:
        pltpu.make_async_remote_copy(
            send2,
            recv2.at[me],
            ssem.at[2],
            rsem.at[2],
            device_id=target(o),
            device_id_type=LOGICAL,
        ).start()
    all_arrived(recv2, recv2, 2).wait_recv()
    total = jnp.sum(recv2[...], axis=0)
    mu = [jnp.broadcast_to(total[:, i : i + 1], (1, N)) for i in range(7)]

    n0 = mu[0]
    a0 = mu[1] / n0
    n1 = mu[2] - a0 * mu[1]
    a1 = (mu[3] - a0 * (mu[2] + n1)) / n1
    b1 = n1 / n0
    c1 = -(a0 + a1)
    c0 = a0 * a1 - b1
    n2 = mu[4] + c1 * mu[3] + c0 * mu[2]
    a2 = (mu[5] + c1 * mu[4] + c0 * mu[3]) / n2 + c1
    b2 = n2 / n1
    square = mu[6] + 2.0 * c1 * mu[5] + (c1 * c1 + 2.0 * c0) * mu[4] + 2.0 * c0 * c1 * mu[3] + c0 * c0 * mu[2]
    n3 = square - (a2 * a2 + b2) * n2
    gammas = [jnp.sqrt(n0), jnp.sqrt(b1), jnp.sqrt(b2), jnp.sqrt(n3 / n2)]
    curvatures = [a0 + 1.0, a1 + 1.0, a2 + 1.0]
    i0, i1, i2 = lax.rsqrt(n0), lax.rsqrt(n1), lax.rsqrt(n2)
    zero = jnp.zeros_like(n0)
    one = jnp.ones_like(n0)
    basis = [(i0, zero, zero), (-a0 * i1, i1, zero), (c0 * i2, c1 * i2, i2)]
    cos_old, cos_now, sin_old, sin_now = one, one, zero, zero
    rhs_scale = gammas[0]
    search_old = search_now = iterate = (zero, zero, zero)
    for k in range(3):
        gamma, gamma_new = gammas[k], gammas[k + 1]
        alpha_zero = cos_now * curvatures[k] - cos_old * sin_now * gamma
        alpha_one = jnp.sqrt(alpha_zero * alpha_zero + gamma_new * gamma_new)
        alpha_two = sin_now * curvatures[k] + cos_old * cos_now * gamma
        alpha_three = sin_old * gamma
        cos_new, sin_new = alpha_zero / alpha_one, gamma_new / alpha_one
        search_new = tuple(
            (z - alpha_three * old - alpha_two * now) / alpha_one
            for z, old, now in zip(basis[k], search_old, search_now)
        )
        iterate = tuple(x + cos_new * rhs_scale * w for x, w in zip(iterate, search_new))
        rhs_scale = -sin_new * rhs_scale
        cos_old, cos_now, sin_old, sin_now = cos_now, cos_new, sin_now, sin_new
        search_old, search_now = search_now, search_new
    factors[...] = jnp.concatenate(list(iterate) + [zero] * 5, axis=0)

    all_arrived(send0, recv0, 0).wait_send()
    all_arrived(send1, recv1, 1).wait_send()
    all_arrived(recv2, recv2, 2).wait_send()
    for i in range(7):
        edge_copy(i).wait_send()
    for phase in range(2):
        for way in range(4):
            halo_copy(phase, way).wait_send()


def combine(pm, fm, factors, out_m, out_f, out_l, om, of, ol, sem):
    x0, x1, x2 = factors[0:1], factors[1:2], factors[2:3]
    stores = [
        pltpu.make_async_copy(om, out_m, sem.at[0]),
        pltpu.make_async_copy(of, out_f, sem.at[1]),
        pltpu.make_async_copy(ol, out_l, sem.at[2]),
    ]
    om[...] = x0 * pm[0] + x1 * pm[1] + x2 * pm[2]
    stores[0].start()
    of[...] = x0 * fm[0] + x1 * fm[1] + x2 * fm[2]
    stores[1].start()
    ol[...] = x1 * fm[3] + x2 * fm[4]
    stores[2].start()
    for store in stores:
        store.wait()


def local(
    rhs_matrix,
    trans_x,
    trans_y,
    leak_matrix,
    rhs_fracture,
    trans_frac,
    store_frac,
    mortar_coef,
    block_home,
    block_len,
    mortar_cell,
    cross_cell,
    cross_partner,
    cross_trans,
):
    tile, block = (ROWS, N), (N, N)
    vmem = lambda shape, kind=F32: pltpu.VMEM(shape, kind)
    results = pl.pallas_call(
        kernel,
        out_shape=(vmem((3,) + tile), vmem((5,) + block), vmem((8, N))),
        in_specs=[pl.BlockSpec(memory_space=pl.ANY)] * 14,
        out_specs=(pl.BlockSpec(memory_space=pltpu.VMEM),) * 3,
        scratch_shapes=[vmem(tile)] * 4
        + [vmem(block)] * 4
        + [vmem((1, N), jnp.int32)] * 3
        + [vmem((2, N), jnp.int32)] * 2
        + [vmem((2, N))]
        + [
            vmem(tile),
            vmem((6,) + tile),
            vmem((N, ROWS0, N)),
            vmem((N, ROWS0, N)),
            vmem((N, ROWS1, N)),
            vmem((N, ROWS1, N)),
            vmem((1, N)),
            vmem((N, 1, N)),
            vmem((2, 2, 1, N)),
            vmem((2, 2, 1, N)),
            vmem((2, 2, 1, ROWS)),
            vmem((2, 2, 1, ROWS)),
            vmem((9, 1, N)),
            vmem((9, 1, N)),
            vmem((5, 1, ROWS)),
            vmem((5, 1, ROWS)),
            pltpu.SemaphoreType.DMA((14,)),
            pltpu.SemaphoreType.DMA((3,)),
            pltpu.SemaphoreType.DMA((3,)),
            pltpu.SemaphoreType.DMA((2, 4)),
            pltpu.SemaphoreType.DMA((2, 4)),
            pltpu.SemaphoreType.DMA((7,)),
            pltpu.SemaphoreType.DMA((7,)),
        ],
        compiler_params=pltpu.CompilerParams(
            collective_id=0, has_side_effects=True, vmem_limit_bytes=60 * 2**20
        ),
    )(
        *[
            pltpu.with_memory_space_constraint(operand, pltpu.HBM)
            for operand in (
                rhs_matrix,
                trans_x,
                trans_y,
                leak_matrix,
                rhs_fracture,
                trans_frac,
                store_frac,
                mortar_coef,
                block_home.T,
                block_len.reshape(1, N),
                mortar_cell.T,
                cross_cell.T,
                cross_partner.T,
                cross_trans.T,
            )
        ]
    )
    return pl.pallas_call(
        combine,
        out_shape=(
            jax.ShapeDtypeStruct(tile, F32),
            jax.ShapeDtypeStruct(block, F32),
            jax.ShapeDtypeStruct(block, F32),
        ),
        in_specs=[pl.BlockSpec(memory_space=pltpu.VMEM)] * 3,
        out_specs=(pl.BlockSpec(memory_space=pl.ANY),) * 3,
        scratch_shapes=[vmem(tile), vmem(block), vmem(block), pltpu.SemaphoreType.DMA((3,))],
    )(*[pltpu.with_memory_space_constraint(result, pltpu.VMEM) for result in results])


def solution(mesh):
    tiles, blocks = P("gx", "gy"), P(("gx", "gy"), None)
    return jax.shard_map(
        local,
        mesh=mesh,
        in_specs=(tiles,) * 4 + (blocks,) * 5 + (P(("gx", "gy")),) + (blocks,) * 4,
        out_specs=(tiles, blocks, blocks),
        check_vma=False,
    )
```

```python
import jax
import jax.numpy as jnp
from jax import lax
from jax.experimental import pallas as pl
from jax.experimental.pallas import tpu as pltpu
from jax.sharding import PartitionSpec as P

LOGICAL = pl.DeviceIdType.LOGICAL
F32 = jnp.float32
BF16 = jnp.bfloat16

N = 128
ROWS = 256
BAND = 64
ROWS0 = 5
ROWS1 = 4
ROWS3 = 6

HOPS = (0, 1, 2, 1)
OFFSETS = sorted(
    (
        (dy, dc, dz, dx)
        for dy in range(4)
        for dc in range(2)
        for dz in range(4)
        for dx in range(4)
        if (dy, dc, dz, dx) != (0, 0, 0, 0)
    ),
    key=lambda o: (-(2 * (HOPS[o[0]] + HOPS[o[2]] + HOPS[o[3]]) + o[1]), o),
)


def split(value):
    high = value.astype(BF16)
    rest = value - high.astype(F32)
    middle = rest.astype(BF16)
    low = (rest - middle.astype(F32)).astype(BF16)
    return [high, middle, low]


def pick(hot, fields):
    if hot.shape[1] == N:
        columns = jnp.concatenate(fields, axis=1)
        stacked = jnp.concatenate(split(columns), axis=0)
        out = jnp.dot(
            jnp.concatenate([hot] * 3, axis=1), stacked, preferred_element_type=F32
        )
        return [out[:, N * i : N * (i + 1)] for i in range(len(fields))]
    parts = [part for field in fields for part in split(field)]
    out = jnp.dot(hot, jnp.concatenate(parts, axis=1), preferred_element_type=F32)
    n = fields[0].shape[1]
    return [
        out[:, 3 * n * i : 3 * n * i + n]
        + out[:, 3 * n * i + n : 3 * n * i + 2 * n]
        + out[:, 3 * n * i + 2 * n : 3 * n * i + 3 * n]
        for i in range(len(fields))
    ]


def fold(value):
    total = value[0:8]
    for i in range(8, value.shape[0], 8):
        total = total + value[i : i + 8]
    return total


def kernel(
    rhs_m_hbm,
    tx_hbm,
    ty_hbm,
    leak_hbm,
    rhs_f_hbm,
    tf_hbm,
    sf_hbm,
    coef_hbm,
    home_hbm,
    len_hbm,
    mcell_hbm,
    cc_hbm,
    cp_hbm,
    ct_hbm,
    pm,
    fm,
    factors,
    rhs_m,
    tx,
    ty,
    leak,
    rhs_f,
    tf,
    sf,
    coef,
    home,
    blen,
    mcell,
    cc,
    cp,
    ct,
    p3_ref,
    co,
    send0,
    recv0,
    send1,
    recv1,
    send2,
    recv2,
    send3,
    recv3,
    hsend_r,
    hrecv_r,
    hsend_c,
    hrecv_c,
    esend_r,
    erecv_r,
    esend_c,
    erecv_c,
    in_sem,
    ssem,
    rsem,
    hs_sem,
    hr_sem,
    es_sem,
    er_sem,
):
    gx = lax.axis_index("gx")
    gy = lax.axis_index("gy")
    me = gx * 16 + gy

    pairs = [
        (len_hbm, blen),
        (home_hbm, home),
        (mcell_hbm, mcell),
        (cc_hbm, cc),
        (cp_hbm, cp),
        (ct_hbm, ct),
        (tf_hbm, tf),
        (sf_hbm, sf),
        (rhs_f_hbm, rhs_f),
        (coef_hbm, coef),
        (tx_hbm, tx),
        (ty_hbm, ty),
        (leak_hbm, leak),
        (rhs_m_hbm, rhs_m),
    ]
    loads = [pltpu.make_async_copy(a, b, in_sem.at[i]) for i, (a, b) in enumerate(pairs)]
    for load in loads:
        load.start()

    ys = [lax.rem(gx // 2 + d, 4) * 32 for d in range(4)]
    cs = [lax.rem(gx + d, 2) * 16 for d in range(2)]
    zs = [lax.rem(gy // 4 + d, 4) * 4 for d in range(4)]
    xs = [lax.rem(gy + d, 4) for d in range(4)]

    def target(o):
        return (ys[o[0]] + cs[o[1]]) + (zs[o[2]] + xs[o[3]])

    barrier = pltpu.get_barrier_semaphore()
    for o in OFFSETS:
        pl.semaphore_signal(barrier, inc=1, device_id=target(o), device_id_type=LOGICAL)

    below = lax.rem(gx + 1, 8) * 16 + gy
    above = lax.rem(gx + 7, 8) * 16 + gy
    right = gx * 16 + lax.rem(gy + 1, 16)
    left = gx * 16 + lax.rem(gy + 15, 16)
    below_right = lax.rem(gx + 1, 8) * 16 + lax.rem(gy + 1, 16)
    above_right = lax.rem(gx + 7, 8) * 16 + lax.rem(gy + 1, 16)
    below_left = lax.rem(gx + 1, 8) * 16 + lax.rem(gy + 15, 16)
    has_above = jnp.where(gx > 0, 1.0, 0.0).astype(F32)
    has_below = jnp.where(gx < 7, 1.0, 0.0).astype(F32)
    has_left = jnp.where(gy > 0, 1.0, 0.0).astype(F32)
    has_right = jnp.where(gy < 15, 1.0, 0.0).astype(F32)

    lane = lax.broadcasted_iota(jnp.int32, (N, N), 1)
    row = lax.broadcasted_iota(jnp.int32, (N, N), 0)

    for load in loads[:6]:
        load.wait()
    lanef = lane.astype(F32)
    len_row = blen[...].astype(F32)
    cp_row = cp[...]
    pb_row = cp_row // N
    pc_row = cp_row - pb_row * N
    table = jnp.concatenate(
        [
            len_row,
            cc[...].astype(F32),
            pb_row.astype(F32),
            pc_row.astype(F32),
            ct[...],
            jnp.zeros((N - 9, N), F32),
        ],
        axis=0,
    ).T
    len_col = table[:, 0:1]
    own_hot = [lanef == table[:, 1 + k : 2 + k] for k in range(2)]
    part_rows = [lanef == table[:, 3 + k : 4 + k] for k in range(2)]
    part_hot = [lanef == table[:, 5 + k : 6 + k] for k in range(2)]
    weight = []
    for k in range(2):
        part_len = jnp.sum(jnp.where(part_rows[k], len_row, 0.0), axis=1, keepdims=True)
        live = (table[:, 1 + k : 2 + k] < len_col) & (table[:, 5 + k : 6 + k] < part_len)
        weight.append(jnp.where(live, table[:, 7 + k : 8 + k], 0.0))
    gather_hot = jnp.concatenate([jnp.where(h, 1.0, 0.0) for h in part_rows], axis=0).astype(BF16)
    spread_hot = jnp.concatenate(
        [jnp.where(row == pb_row[k : k + 1], 1.0, 0.0) for k in range(2)], axis=1
    ).astype(BF16)

    def spread(own_values, part_values):
        pieces = jnp.concatenate(
            [jnp.where(part_hot[k], part_values[k], 0.0) for k in range(2)], axis=0
        )
        out = pick(spread_hot, [pieces])[0]
        for k in range(2):
            out = out + jnp.where(own_hot[k], own_values[k], 0.0)
        return out

    for load in loads[6:10]:
        load.wait()
    mask = jnp.where(lanef < len_col, 1.0, 0.0)
    face = jnp.where(lanef + 1.0 < len_col, tf[...], 0.0)
    face_prev = pltpu.roll(face, 1, 1)
    diag_f = sf[...] * mask + face + face_prev + spread(weight, weight)
    safe = diag_f + 1.0 - mask
    inv_f = mask / safe
    metric_l = 1.0 / coef[...] + 1.0 / safe
    inv_l = mask / metric_l
    ratio_l = inv_l / coef[...]
    q0 = inv_f * rhs_f[...]

    def off_f(q):
        rows = pick(gather_hot, [q])[0]
        part = [
            jnp.sum(jnp.where(part_hot[k], rows[k * N : k * N + N], 0.0), axis=1, keepdims=True)
            for k in range(2)
        ]
        own = [jnp.sum(jnp.where(own_hot[k], q, 0.0), axis=1, keepdims=True) for k in range(2)]
        crossing = spread(
            [weight[k] * part[k] for k in range(2)], [weight[k] * own[k] for k in range(2)]
        )
        return face * pltpu.roll(q, N - 1, 1) + face_prev * pltpu.roll(q, 1, 1) + crossing

    q1 = -inv_f * off_f(q0)

    home_hit = row == home[...]
    first = jnp.min(jnp.where(home_hit, lanef, 1e3), axis=1, keepdims=True)
    last = jnp.max(jnp.where(home_hit, lanef, -1.0), axis=1, keepdims=True)
    slots = [
        jnp.where(lanef == first, 1.0, 0.0),
        jnp.where((lanef == last) & (last > first), 1.0, 0.0),
    ]
    mcell_row = mcell[...].astype(F32)
    cells = [jnp.sum(s * mcell_row, axis=1, keepdims=True) for s in slots]
    slot_hot = jnp.concatenate(slots, axis=0).astype(BF16)
    q2_part = -inv_f * off_f(q1)
    packed = pick(slot_hot, [inv_l, q0, ratio_l, q1, q2_part])
    for i, value in enumerate(packed[:2]):
        send0[:, 2 * i, :] = value[:N]
        send0[:, 2 * i + 1, :] = value[N:]
    send0[:, 4, :] = jnp.where(lane < BAND, cells[0], cells[1])
    for i, value in enumerate(packed[2:]):
        send3[:, 2 * i, :] = value[:N]
        send3[:, 2 * i + 1, :] = value[N:]
    recv0[pl.ds(me, 1)] = send0[pl.ds(me, 1)]
    recv3[pl.ds(me, 1)] = send3[pl.ds(me, 1)]

    fm[0] = q0
    fm[1] = q1

    for load in loads[10:]:
        load.wait()
    sub8 = lax.broadcasted_iota(jnp.int32, (8, N), 0)
    lane8 = lax.broadcasted_iota(jnp.int32, (8, N), 1)
    ends = jnp.where(
        ((sub8 == 0) & (lane8 == 0)) | ((sub8 == 1) & (lane8 == N - 1)), 1.0, 0.0
    ).astype(BF16)

    def end_cols(field):
        return lax.dot_general(
            jnp.concatenate([ends] * 3, axis=1),
            jnp.concatenate(split(field), axis=1),
            (((1,), (1,)), ((), ())),
            preferred_element_type=F32,
        )

    def halo_copy(phase, way):
        device = (below, above, right, left)[way]
        send, recv = (hsend_r, hrecv_r) if way < 2 else (hsend_c, hrecv_c)
        return pltpu.make_async_remote_copy(
            send.at[phase, way % 2],
            recv.at[phase, way % 2],
            hs_sem.at[phase, way],
            hr_sem.at[phase, way],
            device_id=device,
            device_id_type=LOGICAL,
        )

    def halo_send(phase, first, last, cols):
        hsend_r[phase, 0] = last
        hsend_r[phase, 1] = first
        hsend_c[phase, 0] = cols[1:2]
        hsend_c[phase, 1] = cols[0:1]
        for way in range(4):
            halo_copy(phase, way).start()

    def as_cols(rows):
        cols = jnp.concatenate(rows + [jnp.zeros((8 - len(rows), ROWS), F32)], axis=0).T
        return [cols[:, k : k + 1] for k in range(len(rows))]

    row_m = lax.broadcasted_iota(jnp.int32, (ROWS, N), 0)
    lane_m = lax.broadcasted_iota(jnp.int32, (ROWS, N), 1)

    def off_m(p, top, bottom, before, after):
        up = jnp.where(row_m == 0, top, pltpu.roll(p, 1, 0))
        down = jnp.where(row_m == ROWS - 1, bottom, pltpu.roll(p, ROWS - 1, 0))
        lft = jnp.where(lane_m == 0, before, pltpu.roll(p, 1, 1))
        rgt = jnp.where(lane_m == N - 1, after, pltpu.roll(p, N - 1, 1))
        return co[0] * down + co[1] * up + co[2] * rgt + co[3] * lft

    def halo(phase):
        for way in range(4):
            halo_copy(phase, way).wait_recv()
        before, after = as_cols([hrecv_c[phase, 0] * has_left, hrecv_c[phase, 1] * has_right])
        return hrecv_r[phase, 0] * has_above, hrecv_r[phase, 1] * has_below, before, after

    tx_up = jnp.where(row_m == 0, 0.0, pltpu.roll(tx[...], 1, 0))
    ty_left = jnp.where(lane_m == 0, 0.0, pltpu.roll(ty[...], 1, 1))
    partial = leak[...] + tx[...] + tx_up + ty[...] + ty_left
    esend_r[0] = tx[ROWS - 1 : ROWS]
    esend_r[1] = rhs_m[ROWS - 1 : ROWS]
    esend_r[2] = partial[ROWS - 1 : ROWS]
    esend_r[3] = rhs_m[0:1]
    esend_r[4] = partial[0:1]
    esend_r[5] = tx[ROWS - 1 : ROWS]
    esend_r[6] = ty[ROWS - 1 : ROWS]
    esend_r[7] = ty[0:1]
    esend_r[8] = tx[ROWS - 1 : ROWS]
    ty_cols, rhs_cols, partial_cols = end_cols(ty[...]), end_cols(rhs_m[...]), end_cols(partial)
    esend_c[0] = ty_cols[1:2]
    esend_c[1] = rhs_cols[1:2]
    esend_c[2] = partial_cols[1:2]
    esend_c[3] = rhs_cols[0:1]
    esend_c[4] = partial_cols[0:1]

    def edge_copy(i):
        send, recv, start, count, device = (
            (esend_r, erecv_r, 0, 3, below),
            (esend_r, erecv_r, 3, 2, above),
            (esend_r, erecv_r, 5, 2, below_right),
            (esend_r, erecv_r, 7, 1, above_right),
            (esend_r, erecv_r, 8, 1, below_left),
            (esend_c, erecv_c, 0, 3, right),
            (esend_c, erecv_c, 3, 2, left),
        )[i]
        return pltpu.make_async_remote_copy(
            send.at[pl.ds(start, count)],
            recv.at[pl.ds(start, count)],
            es_sem.at[i],
            er_sem.at[i],
            device_id=device,
            device_id_type=LOGICAL,
        )

    pl.semaphore_wait(barrier, N - 1)
    for i in range(7):
        edge_copy(i).start()

    def send_to(o, send, recv, i):
        t = target(o)
        pltpu.make_async_remote_copy(
            send.at[t],
            recv.at[me],
            ssem.at[i],
            rsem.at[i],
            device_id=t,
            device_id_type=LOGICAL,
        ).start()

    for o in OFFSETS:
        send_to(o, send0, recv0, 0)

    for i in range(7):
        edge_copy(i).wait_recv()
    lane_1 = lax.broadcasted_iota(jnp.int32, (1, N), 1)

    def corner(value, factor):
        return jnp.where(lane_1 == 0, value, 0.0) * factor

    def corner_col(value, factor):
        return jnp.concatenate([corner(value, factor), jnp.zeros((1, N), F32)], axis=1)

    diag_above = erecv_r[2] + corner(pltpu.roll(erecv_r[6], 1, 1), has_left)
    diag_below = erecv_r[4] + tx[ROWS - 1 : ROWS] + corner(pltpu.roll(erecv_r[7], 1, 1), has_left)
    diag_left = erecv_c[2] + corner_col(pltpu.roll(erecv_r[5], 1, 1), has_above)
    diag_right = erecv_c[4] + esend_c[0] + corner_col(erecv_r[8], has_above)
    p0_above = erecv_r[1] / diag_above * has_above
    p0_below = erecv_r[3] / diag_below * has_below
    ty_col, p0_left, p0_right = as_cols(
        [
            erecv_c[0] * has_left,
            erecv_c[1] / diag_left * has_left,
            erecv_c[3] / diag_right * has_right,
        ]
    )
    tx_prev = jnp.where(row_m == 0, erecv_r[0] * has_above, pltpu.roll(tx[...], 1, 0))
    ty_prev = jnp.where(lane_m == 0, ty_col, pltpu.roll(ty[...], 1, 1))
    diag_m = leak[...] + tx[...] + tx_prev + ty[...] + ty_prev
    inv_m = 1.0 / diag_m
    pm[0] = rhs_m[...] * inv_m
    co[0] = tx[...] * inv_m
    co[1] = tx_prev * inv_m
    co[2] = ty[...] * inv_m
    co[3] = ty_prev * inv_m
    co[4] = diag_m
    co[5] = inv_m
    p1 = -off_m(pm[0], p0_above, p0_below, p0_left, p0_right)
    halo_send(0, p1[0:1], p1[ROWS - 1 : ROWS], end_cols(p1))
    pm[1] = p1
    for o in OFFSETS:
        send_to(o, send3, recv3, 3)

    slot_hot_t = jnp.concatenate([s.T for s in slots], axis=1).astype(BF16)
    dm = co[4]
    moments = [
        fold(dm * pm[0] * pm[0]) + fold(safe * fm[0] * fm[0]),
        fold(dm * pm[0] * pm[1]) + fold(safe * fm[0] * fm[1]),
        fold(dm * pm[1] * pm[1]) + fold(safe * fm[1] * fm[1]),
    ]

    def all_arrived(send, recv, i):
        return pltpu.make_async_remote_copy(
            send.at[pl.ds(0, N - 1)],
            recv.at[pl.ds(0, N - 1)],
            ssem.at[i],
            rsem.at[i],
            device_id=right,
            device_id_type=LOGICAL,
        )

    all_arrived(send0, recv0, 0).wait_recv()
    lane_band = jnp.where(lane < BAND, lane, lane - BAND).astype(F32)
    hit = jnp.where(recv0[:, 4, :] == lane_band, 1.0, 0.0)
    hit_slots = jnp.concatenate(
        [jnp.where(lane < BAND, hit, 0.0), jnp.where(lane < BAND, 0.0, hit)], axis=0
    ).astype(BF16)

    def sample(fields):
        return pick(hit_slots, [jnp.concatenate([f, f], axis=0) for f in fields])

    p0_at, p1_at = sample([pm[0, 0:BAND], pm[1, 0:BAND]])
    for i, value in enumerate((p0_at, p1_at)):
        send1[:, 2 * i, :] = value[:N]
        send1[:, 2 * i + 1, :] = value[N:]
    recv1[pl.ds(me, 1)] = send1[pl.ds(me, 1)]
    for o in OFFSETS:
        send_to(o, send1, recv1, 1)

    hit_t = hit.T
    hit_rows = jnp.concatenate([hit_t[:BAND], hit_t[BAND:]], axis=1).astype(BF16)

    def both(ref, r):
        return jnp.concatenate([ref[:, r, :], ref[:, r + 1, :]], axis=0)

    inv_at = both(recv0, 0)
    l1 = inv_at * (p0_at - both(recv0, 2))
    p2_part = -off_m(pm[1], *halo(0))
    part_cols = end_cols(p2_part)
    pushed = co[5, 0:BAND] * pick(hit_rows, [l1])[0]
    pm[2] = p2_part
    pm[2, 0:BAND] += pushed
    pushed_cols = jnp.concatenate(
        [end_cols(pushed), jnp.zeros((8, ROWS - BAND), F32)], axis=1
    )
    halo_send(
        1,
        p2_part[0:1] + pushed[0:1],
        p2_part[ROWS - 1 : ROWS],
        part_cols + pushed_cols,
    )
    p2 = pm[2]
    p2_at = sample([p2[0:BAND]])[0]
    all_arrived(send3, recv3, 3).wait_recv()
    ratio_at = both(recv3, 0)
    l2 = inv_at * (p1_at - both(recv3, 2)) - (1.0 + ratio_at) * l1
    l3 = inv_at * (p2_at - both(recv3, 4)) + (1.0 - ratio_at) * l1 - (1.0 + ratio_at) * l2
    metric_at = jnp.where(inv_at > 0.0, 1.0 / inv_at, 0.0)
    m1, m2 = metric_at * l1, metric_at * l2
    moments[2] += fold(m1 * l1)
    moments.append(fold(m1 * l2))
    moments.append(fold(m2 * l2))
    moments.append(fold(m2 * l3))
    moments.append(fold(metric_at * l3 * l3))
    d2 = co[4] * pm[2]
    moments[3] += fold(d2 * pm[1])
    moments[4] += fold(d2 * pm[2])
    p3_ref[...] = -off_m(pm[2], *halo(1))
    p3_ref[0:BAND] += co[5, 0:BAND] * pick(hit_rows, [l2])[0]
    p3 = p3_ref[...]
    moments[5] += fold(d2 * p3)
    moments[6] += fold(co[4] * p3 * p3)

    all_arrived(send1, recv1, 1).wait_recv()

    def returned(r):
        return jnp.concatenate([recv1[:, r, :], recv1[:, r + 1, :]], axis=0)

    p0_at, p1_at = pick(slot_hot_t, [returned(0), returned(2)])
    l1 = inv_l * (p0_at - fm[0])
    l2 = inv_l * (p1_at - fm[1]) - (1.0 + ratio_l) * l1
    q2 = q2_part - inv_f * l1
    q3 = -inv_f * (off_f(q2) + l2)
    fm[2] = q2
    fm[3] = l1
    fm[4] = l2
    s2 = safe * q2
    moments[3] += fold(s2 * fm[1])
    moments[4] += fold(s2 * q2)
    moments[5] += fold(s2 * q3)
    moments[6] += fold(safe * q3 * q3)
    rows = [jnp.sum(m, axis=0, keepdims=True) for m in moments]
    sums = jnp.sum(jnp.concatenate(rows + [jnp.zeros((1, N), F32)], axis=0), axis=1, keepdims=True)
    mine = jnp.sum(jnp.where(lane8 == sub8, sums, 0.0), axis=0, keepdims=True)
    send2[0:1] = mine
    recv2[pl.ds(me, 1), 0:1] = mine[None]
    for o in OFFSETS:
        pltpu.make_async_remote_copy(
            send2.at[0:1],
            recv2.at[me, 0:1],
            ssem.at[2],
            rsem.at[2],
            device_id=target(o),
            device_id_type=LOGICAL,
        ).start()
    all_arrived(recv2.at[:, 0:1], recv2.at[:, 0:1], 2).wait_recv()
    total = jnp.sum(fold(recv2[:, 0, :]), axis=0, keepdims=True)
    mu = [jnp.broadcast_to(total[:, i : i + 1], (1, N)) for i in range(7)]

    gram = [mu[k] + 2.0 * mu[k + 1] + mu[k + 2] for k in range(5)]
    right_side = [mu[k] + mu[k + 1] for k in range(3)]
    i0 = 1.0 / gram[0]
    l10, l20 = gram[1] * i0, gram[2] * i0
    i1 = 1.0 / (gram[2] - l10 * gram[1])
    off = gram[3] - l20 * gram[1]
    l21 = off * i1
    i2 = 1.0 / (gram[4] - l20 * gram[2] - l21 * off)
    y1 = right_side[1] - l10 * right_side[0]
    y2 = right_side[2] - l20 * right_side[0] - l21 * y1
    x2 = y2 * i2
    x1 = y1 * i1 - l21 * x2
    x0 = right_side[0] * i0 - l10 * x1 - l20 * x2
    factors[...] = jnp.concatenate([x0, x1, x2, jnp.zeros((5, N), F32)], axis=0)

    all_arrived(send0, recv0, 0).wait_send()
    all_arrived(send1, recv1, 1).wait_send()
    all_arrived(recv2.at[:, 0:1], recv2.at[:, 0:1], 2).wait_send()
    all_arrived(send3, recv3, 3).wait_send()
    for i in range(7):
        edge_copy(i).wait_send()
    for phase in range(2):
        for way in range(4):
            halo_copy(phase, way).wait_send()


def combine(pm, fm, factors, out_m, out_f, out_l, om, of, ol, sem):
    x0, x1, x2 = factors[0:1], factors[1:2], factors[2:3]
    stores = [
        pltpu.make_async_copy(om, out_m, sem.at[0]),
        pltpu.make_async_copy(of, out_f, sem.at[1]),
        pltpu.make_async_copy(ol, out_l, sem.at[2]),
    ]
    om[...] = x0 * pm[0] + x1 * pm[1] + x2 * pm[2]
    stores[0].start()
    of[...] = x0 * fm[0] + x1 * fm[1] + x2 * fm[2]
    stores[1].start()
    ol[...] = x1 * fm[3] + x2 * fm[4]
    stores[2].start()
    for store in stores:
        store.wait()


def local(
    rhs_matrix,
    trans_x,
    trans_y,
    leak_matrix,
    rhs_fracture,
    trans_frac,
    store_frac,
    mortar_coef,
    block_home,
    block_len,
    mortar_cell,
    cross_cell,
    cross_partner,
    cross_trans,
):
    tile, block = (ROWS, N), (N, N)
    vmem = lambda shape, kind=F32: pltpu.VMEM(shape, kind)
    results = pl.pallas_call(
        kernel,
        out_shape=(vmem((3,) + tile), vmem((5,) + block), vmem((8, N))),
        in_specs=[pl.BlockSpec(memory_space=pl.ANY)] * 14,
        out_specs=(pl.BlockSpec(memory_space=pltpu.VMEM),) * 3,
        scratch_shapes=[vmem(tile)] * 4
        + [vmem(block)] * 4
        + [vmem((1, N), jnp.int32)] * 3
        + [vmem((2, N), jnp.int32)] * 2
        + [vmem((2, N))]
        + [
            vmem(tile),
            vmem((6,) + tile),
            vmem((N, ROWS0, N)),
            vmem((N, ROWS0, N)),
            vmem((N, ROWS1, N)),
            vmem((N, ROWS1, N)),
            vmem((8, N)),
            vmem((N, 8, N)),
            vmem((N, ROWS3, N)),
            vmem((N, ROWS3, N)),
            vmem((2, 2, 1, N)),
            vmem((2, 2, 1, N)),
            vmem((2, 2, 1, ROWS)),
            vmem((2, 2, 1, ROWS)),
            vmem((9, 1, N)),
            vmem((9, 1, N)),
            vmem((5, 1, ROWS)),
            vmem((5, 1, ROWS)),
            pltpu.SemaphoreType.DMA((14,)),
            pltpu.SemaphoreType.DMA((4,)),
            pltpu.SemaphoreType.DMA((4,)),
            pltpu.SemaphoreType.DMA((2, 4)),
            pltpu.SemaphoreType.DMA((2, 4)),
            pltpu.SemaphoreType.DMA((7,)),
            pltpu.SemaphoreType.DMA((7,)),
        ],
        compiler_params=pltpu.CompilerParams(
            collective_id=0, has_side_effects=True, vmem_limit_bytes=60 * 2**20
        ),
    )(
        *[
            pltpu.with_memory_space_constraint(operand, pltpu.HBM)
            for operand in (
                rhs_matrix,
                trans_x,
                trans_y,
                leak_matrix,
                rhs_fracture,
                trans_frac,
                store_frac,
                mortar_coef,
                block_home.T,
                block_len.reshape(1, N),
                mortar_cell.T,
                cross_cell.T,
                cross_partner.T,
                cross_trans.T,
            )
        ]
    )
    return pl.pallas_call(
        combine,
        out_shape=(
            jax.ShapeDtypeStruct(tile, F32),
            jax.ShapeDtypeStruct(block, F32),
            jax.ShapeDtypeStruct(block, F32),
        ),
        in_specs=[pl.BlockSpec(memory_space=pltpu.VMEM)] * 3,
        out_specs=(pl.BlockSpec(memory_space=pl.ANY),) * 3,
        scratch_shapes=[vmem(tile), vmem(block), vmem(block), pltpu.SemaphoreType.DMA((3,))],
    )(*[pltpu.with_memory_space_constraint(result, pltpu.VMEM) for result in results])


def solution(mesh):
    tiles, blocks = P("gx", "gy"), P(("gx", "gy"), None)
    return jax.shard_map(
        local,
        mesh=mesh,
        in_specs=(tiles,) * 4 + (blocks,) * 5 + (P(("gx", "gy")),) + (blocks,) * 4,
        out_specs=(tiles, blocks, blocks),
        check_vma=False,
    )
```

```python
import jax
import jax.numpy as jnp
from jax import lax
from jax.experimental import pallas as pl
from jax.experimental.pallas import tpu as pltpu
from jax.sharding import PartitionSpec as P

LOGICAL = pl.DeviceIdType.LOGICAL
F32 = jnp.float32
BF16 = jnp.bfloat16

N = 128
ROWS = 256
BAND = 64
ROWS0 = 5
ROWS1 = 4
ROWS3 = 4
ROWS4 = 2

HOPS = (0, 1, 2, 1)
OFFSETS = sorted(
    (
        (dy, dc, dz, dx)
        for dy in range(4)
        for dc in range(2)
        for dz in range(4)
        for dx in range(4)
        if (dy, dc, dz, dx) != (0, 0, 0, 0)
    ),
    key=lambda o: (-(2 * (HOPS[o[0]] + HOPS[o[2]] + HOPS[o[3]]) + o[1]), o),
)


def split(value):
    high = value.astype(BF16)
    rest = value - high.astype(F32)
    middle = rest.astype(BF16)
    low = (rest - middle.astype(F32)).astype(BF16)
    return [high, middle, low]


def pick(hot, fields):
    if hot.shape[1] == N:
        columns = jnp.concatenate(fields, axis=1)
        stacked = jnp.concatenate(split(columns), axis=0)
        out = jnp.dot(
            jnp.concatenate([hot] * 3, axis=1), stacked, preferred_element_type=F32
        )
        return [out[:, N * i : N * (i + 1)] for i in range(len(fields))]
    parts = [part for field in fields for part in split(field)]
    out = jnp.dot(hot, jnp.concatenate(parts, axis=1), preferred_element_type=F32)
    n = fields[0].shape[1]
    return [
        out[:, 3 * n * i : 3 * n * i + n]
        + out[:, 3 * n * i + n : 3 * n * i + 2 * n]
        + out[:, 3 * n * i + 2 * n : 3 * n * i + 3 * n]
        for i in range(len(fields))
    ]


def fold(value):
    total = value[0:8]
    for i in range(8, value.shape[0], 8):
        total = total + value[i : i + 8]
    return total


def kernel(
    rhs_m_hbm,
    tx_hbm,
    ty_hbm,
    leak_hbm,
    rhs_f_hbm,
    tf_hbm,
    sf_hbm,
    coef_hbm,
    home_hbm,
    len_hbm,
    mcell_hbm,
    cc_hbm,
    cp_hbm,
    ct_hbm,
    pm,
    fm,
    factors,
    rhs_m,
    tx,
    ty,
    leak,
    rhs_f,
    tf,
    sf,
    coef,
    home,
    blen,
    mcell,
    cc,
    cp,
    ct,
    p3_ref,
    co,
    send0,
    recv0,
    send1,
    recv1,
    send2,
    recv2,
    send3,
    recv3,
    send4,
    recv4,
    hsend_r,
    hrecv_r,
    hsend_c,
    hrecv_c,
    esend_r,
    erecv_r,
    esend_c,
    erecv_c,
    in_sem,
    ssem,
    rsem,
    hs_sem,
    hr_sem,
    es_sem,
    er_sem,
):
    gx = lax.axis_index("gx")
    gy = lax.axis_index("gy")
    me = gx * 16 + gy

    pairs = [
        (len_hbm, blen),
        (home_hbm, home),
        (mcell_hbm, mcell),
        (cc_hbm, cc),
        (cp_hbm, cp),
        (ct_hbm, ct),
        (tf_hbm, tf),
        (sf_hbm, sf),
        (rhs_f_hbm, rhs_f),
        (coef_hbm, coef),
        (tx_hbm, tx),
        (ty_hbm, ty),
        (leak_hbm, leak),
        (rhs_m_hbm, rhs_m),
    ]
    loads = [pltpu.make_async_copy(a, b, in_sem.at[i]) for i, (a, b) in enumerate(pairs)]
    for load in loads:
        load.start()

    ys = [lax.rem(gx // 2 + d, 4) * 32 for d in range(4)]
    cs = [lax.rem(gx + d, 2) * 16 for d in range(2)]
    zs = [lax.rem(gy // 4 + d, 4) * 4 for d in range(4)]
    xs = [lax.rem(gy + d, 4) for d in range(4)]

    def target(o):
        return (ys[o[0]] + cs[o[1]]) + (zs[o[2]] + xs[o[3]])

    barrier = pltpu.get_barrier_semaphore()
    for o in OFFSETS:
        pl.semaphore_signal(barrier, inc=1, device_id=target(o), device_id_type=LOGICAL)

    below = lax.rem(gx + 1, 8) * 16 + gy
    above = lax.rem(gx + 7, 8) * 16 + gy
    right = gx * 16 + lax.rem(gy + 1, 16)
    left = gx * 16 + lax.rem(gy + 15, 16)
    below_right = lax.rem(gx + 1, 8) * 16 + lax.rem(gy + 1, 16)
    above_right = lax.rem(gx + 7, 8) * 16 + lax.rem(gy + 1, 16)
    below_left = lax.rem(gx + 1, 8) * 16 + lax.rem(gy + 15, 16)
    has_above = jnp.where(gx > 0, 1.0, 0.0).astype(F32)
    has_below = jnp.where(gx < 7, 1.0, 0.0).astype(F32)
    has_left = jnp.where(gy > 0, 1.0, 0.0).astype(F32)
    has_right = jnp.where(gy < 15, 1.0, 0.0).astype(F32)

    lane = lax.broadcasted_iota(jnp.int32, (N, N), 1)
    row = lax.broadcasted_iota(jnp.int32, (N, N), 0)

    for load in loads[:6]:
        load.wait()
    lanef = lane.astype(F32)
    len_row = blen[...].astype(F32)
    cp_row = cp[...]
    pb_row = cp_row // N
    pc_row = cp_row - pb_row * N
    table = jnp.concatenate(
        [
            len_row,
            cc[...].astype(F32),
            pb_row.astype(F32),
            pc_row.astype(F32),
            ct[...],
            jnp.zeros((N - 9, N), F32),
        ],
        axis=0,
    ).T
    len_col = table[:, 0:1]
    own_hot = [lanef == table[:, 1 + k : 2 + k] for k in range(2)]
    part_rows = [lanef == table[:, 3 + k : 4 + k] for k in range(2)]
    part_hot = [lanef == table[:, 5 + k : 6 + k] for k in range(2)]
    weight = []
    for k in range(2):
        part_len = jnp.sum(jnp.where(part_rows[k], len_row, 0.0), axis=1, keepdims=True)
        live = (table[:, 1 + k : 2 + k] < len_col) & (table[:, 5 + k : 6 + k] < part_len)
        weight.append(jnp.where(live, table[:, 7 + k : 8 + k], 0.0))
    gather_hot = jnp.concatenate([jnp.where(h, 1.0, 0.0) for h in part_rows], axis=0).astype(BF16)
    spread_hot = jnp.concatenate(
        [jnp.where(row == pb_row[k : k + 1], 1.0, 0.0) for k in range(2)], axis=1
    ).astype(BF16)

    def spread(own_values, part_values):
        pieces = jnp.concatenate(
            [jnp.where(part_hot[k], part_values[k], 0.0) for k in range(2)], axis=0
        )
        out = pick(spread_hot, [pieces])[0]
        for k in range(2):
            out = out + jnp.where(own_hot[k], own_values[k], 0.0)
        return out

    for load in loads[6:10]:
        load.wait()
    mask = jnp.where(lanef < len_col, 1.0, 0.0)
    face = jnp.where(lanef + 1.0 < len_col, tf[...], 0.0)
    face_prev = pltpu.roll(face, 1, 1)
    diag_f = sf[...] * mask + face + face_prev + spread(weight, weight)
    safe = diag_f + 1.0 - mask
    inv_f = mask / safe
    metric_l = 1.0 / coef[...] + 1.0 / safe
    inv_l = mask / metric_l
    ratio_l = inv_l / coef[...]
    q0 = inv_f * rhs_f[...]

    def off_f(q):
        rows = pick(gather_hot, [q])[0]
        part = [
            jnp.sum(jnp.where(part_hot[k], rows[k * N : k * N + N], 0.0), axis=1, keepdims=True)
            for k in range(2)
        ]
        own = [jnp.sum(jnp.where(own_hot[k], q, 0.0), axis=1, keepdims=True) for k in range(2)]
        crossing = spread(
            [weight[k] * part[k] for k in range(2)], [weight[k] * own[k] for k in range(2)]
        )
        return face * pltpu.roll(q, N - 1, 1) + face_prev * pltpu.roll(q, 1, 1) + crossing

    q1 = -inv_f * off_f(q0)

    home_hit = row == home[...]
    first = jnp.min(jnp.where(home_hit, lanef, 1e3), axis=1, keepdims=True)
    last = jnp.max(jnp.where(home_hit, lanef, -1.0), axis=1, keepdims=True)
    slots = [
        jnp.where(lanef == first, 1.0, 0.0),
        jnp.where((lanef == last) & (last > first), 1.0, 0.0),
    ]
    mcell_row = mcell[...].astype(F32)
    cells = [jnp.sum(s * mcell_row, axis=1, keepdims=True) for s in slots]
    slot_hot = jnp.concatenate(slots, axis=0).astype(BF16)
    q2_part = -inv_f * off_f(q1)
    packed = pick(slot_hot, [inv_l, q0, ratio_l, q1, q2_part])
    for i, value in enumerate(packed[:2]):
        send0[:, 2 * i, :] = value[:N]
        send0[:, 2 * i + 1, :] = value[N:]
    send0[:, 4, :] = jnp.where(lane < BAND, cells[0], cells[1])
    send4[:, 0, :] = packed[4][:N]
    send4[:, 1, :] = packed[4][N:]
    for i, value in enumerate(packed[2:4]):
        send3[:, 2 * i, :] = value[:N]
        send3[:, 2 * i + 1, :] = value[N:]
    recv0[pl.ds(me, 1)] = send0[pl.ds(me, 1)]
    recv3[pl.ds(me, 1)] = send3[pl.ds(me, 1)]
    recv4[pl.ds(me, 1)] = send4[pl.ds(me, 1)]

    fm[0] = q0
    fm[1] = q1

    for load in loads[10:]:
        load.wait()
    sub8 = lax.broadcasted_iota(jnp.int32, (8, N), 0)
    lane8 = lax.broadcasted_iota(jnp.int32, (8, N), 1)
    ends = jnp.where(
        ((sub8 == 0) & (lane8 == 0)) | ((sub8 == 1) & (lane8 == N - 1)), 1.0, 0.0
    ).astype(BF16)

    def end_cols(field):
        return lax.dot_general(
            jnp.concatenate([ends] * 3, axis=1),
            jnp.concatenate(split(field), axis=1),
            (((1,), (1,)), ((), ())),
            preferred_element_type=F32,
        )

    def halo_copy(phase, way):
        device = (below, above, right, left)[way]
        send, recv = (hsend_r, hrecv_r) if way < 2 else (hsend_c, hrecv_c)
        return pltpu.make_async_remote_copy(
            send.at[phase, way % 2],
            recv.at[phase, way % 2],
            hs_sem.at[phase, way],
            hr_sem.at[phase, way],
            device_id=device,
            device_id_type=LOGICAL,
        )

    def halo_send(phase, first, last, cols):
        hsend_r[phase, 0] = last
        hsend_r[phase, 1] = first
        hsend_c[phase, 0] = cols[1:2]
        hsend_c[phase, 1] = cols[0:1]
        for way in range(4):
            halo_copy(phase, way).start()

    def as_cols(rows):
        cols = jnp.concatenate(rows + [jnp.zeros((8 - len(rows), ROWS), F32)], axis=0).T
        return [cols[:, k : k + 1] for k in range(len(rows))]

    row_m = lax.broadcasted_iota(jnp.int32, (ROWS, N), 0)
    lane_m = lax.broadcasted_iota(jnp.int32, (ROWS, N), 1)

    def off_m(p, top, bottom, before, after):
        up = jnp.where(row_m == 0, top, pltpu.roll(p, 1, 0))
        down = jnp.where(row_m == ROWS - 1, bottom, pltpu.roll(p, ROWS - 1, 0))
        lft = jnp.where(lane_m == 0, before, pltpu.roll(p, 1, 1))
        rgt = jnp.where(lane_m == N - 1, after, pltpu.roll(p, N - 1, 1))
        return co[0] * down + co[1] * up + co[2] * rgt + co[3] * lft

    def halo(phase):
        for way in range(4):
            halo_copy(phase, way).wait_recv()
        before, after = as_cols([hrecv_c[phase, 0] * has_left, hrecv_c[phase, 1] * has_right])
        return hrecv_r[phase, 0] * has_above, hrecv_r[phase, 1] * has_below, before, after

    tx_up = jnp.where(row_m == 0, 0.0, pltpu.roll(tx[...], 1, 0))
    ty_left = jnp.where(lane_m == 0, 0.0, pltpu.roll(ty[...], 1, 1))
    partial = leak[...] + tx[...] + tx_up + ty[...] + ty_left
    esend_r[0] = tx[ROWS - 1 : ROWS]
    esend_r[1] = rhs_m[ROWS - 1 : ROWS]
    esend_r[2] = partial[ROWS - 1 : ROWS]
    esend_r[3] = rhs_m[0:1]
    esend_r[4] = partial[0:1]
    esend_r[5] = tx[ROWS - 1 : ROWS]
    esend_r[6] = ty[ROWS - 1 : ROWS]
    esend_r[7] = ty[0:1]
    esend_r[8] = tx[ROWS - 1 : ROWS]
    ty_cols, rhs_cols, partial_cols = end_cols(ty[...]), end_cols(rhs_m[...]), end_cols(partial)
    esend_c[0] = ty_cols[1:2]
    esend_c[1] = rhs_cols[1:2]
    esend_c[2] = partial_cols[1:2]
    esend_c[3] = rhs_cols[0:1]
    esend_c[4] = partial_cols[0:1]

    def edge_copy(i):
        send, recv, start, count, device = (
            (esend_r, erecv_r, 0, 3, below),
            (esend_r, erecv_r, 3, 2, above),
            (esend_r, erecv_r, 5, 2, below_right),
            (esend_r, erecv_r, 7, 1, above_right),
            (esend_r, erecv_r, 8, 1, below_left),
            (esend_c, erecv_c, 0, 3, right),
            (esend_c, erecv_c, 3, 2, left),
        )[i]
        return pltpu.make_async_remote_copy(
            send.at[pl.ds(start, count)],
            recv.at[pl.ds(start, count)],
            es_sem.at[i],
            er_sem.at[i],
            device_id=device,
            device_id_type=LOGICAL,
        )

    pl.semaphore_wait(barrier, N - 1)
    for i in range(7):
        edge_copy(i).start()

    def send_to(o, send, recv, i):
        t = target(o)
        pltpu.make_async_remote_copy(
            send.at[t],
            recv.at[me],
            ssem.at[i],
            rsem.at[i],
            device_id=t,
            device_id_type=LOGICAL,
        ).start()

    for o in OFFSETS:
        send_to(o, send0, recv0, 0)

    for i in range(7):
        edge_copy(i).wait_recv()
    lane_1 = lax.broadcasted_iota(jnp.int32, (1, N), 1)

    def corner(value, factor):
        return jnp.where(lane_1 == 0, value, 0.0) * factor

    def corner_col(value, factor):
        return jnp.concatenate([corner(value, factor), jnp.zeros((1, N), F32)], axis=1)

    diag_above = erecv_r[2] + corner(pltpu.roll(erecv_r[6], 1, 1), has_left)
    diag_below = erecv_r[4] + tx[ROWS - 1 : ROWS] + corner(pltpu.roll(erecv_r[7], 1, 1), has_left)
    diag_left = erecv_c[2] + corner_col(pltpu.roll(erecv_r[5], 1, 1), has_above)
    diag_right = erecv_c[4] + esend_c[0] + corner_col(erecv_r[8], has_above)
    p0_above = erecv_r[1] / diag_above * has_above
    p0_below = erecv_r[3] / diag_below * has_below
    ty_col, p0_left, p0_right = as_cols(
        [
            erecv_c[0] * has_left,
            erecv_c[1] / diag_left * has_left,
            erecv_c[3] / diag_right * has_right,
        ]
    )
    tx_prev = jnp.where(row_m == 0, erecv_r[0] * has_above, pltpu.roll(tx[...], 1, 0))
    ty_prev = jnp.where(lane_m == 0, ty_col, pltpu.roll(ty[...], 1, 1))
    diag_m = leak[...] + tx[...] + tx_prev + ty[...] + ty_prev
    inv_m = 1.0 / diag_m
    pm[0] = rhs_m[...] * inv_m
    co[0] = tx[...] * inv_m
    co[1] = tx_prev * inv_m
    co[2] = ty[...] * inv_m
    co[3] = ty_prev * inv_m
    co[4] = diag_m
    co[5] = inv_m
    p1 = -off_m(pm[0], p0_above, p0_below, p0_left, p0_right)
    halo_send(0, p1[0:1], p1[ROWS - 1 : ROWS], end_cols(p1))
    pm[1] = p1
    for o in OFFSETS:
        send_to(o, send3, recv3, 3)

    slot_hot_t = jnp.concatenate([s.T for s in slots], axis=1).astype(BF16)
    dm = co[4]
    moments = [
        fold(dm * pm[0] * pm[0]) + fold(safe * fm[0] * fm[0]),
        fold(dm * pm[0] * pm[1]) + fold(safe * fm[0] * fm[1]),
        fold(dm * pm[1] * pm[1]) + fold(safe * fm[1] * fm[1]),
    ]

    def all_arrived(send, recv, i):
        return pltpu.make_async_remote_copy(
            send.at[pl.ds(0, N - 1)],
            recv.at[pl.ds(0, N - 1)],
            ssem.at[i],
            rsem.at[i],
            device_id=right,
            device_id_type=LOGICAL,
        )

    all_arrived(send0, recv0, 0).wait_recv()
    lane_band = jnp.where(lane < BAND, lane, lane - BAND).astype(F32)
    hit = jnp.where(recv0[:, 4, :] == lane_band, 1.0, 0.0)
    hit_slots = jnp.concatenate(
        [jnp.where(lane < BAND, hit, 0.0), jnp.where(lane < BAND, 0.0, hit)], axis=0
    ).astype(BF16)

    def sample(fields):
        return pick(hit_slots, [jnp.concatenate([f, f], axis=0) for f in fields])

    p0_at, p1_at = sample([pm[0, 0:BAND], pm[1, 0:BAND]])
    for i, value in enumerate((p0_at, p1_at)):
        send1[:, 2 * i, :] = value[:N]
        send1[:, 2 * i + 1, :] = value[N:]
    recv1[pl.ds(me, 1)] = send1[pl.ds(me, 1)]
    for o in OFFSETS:
        send_to(o, send1, recv1, 1)

    hit_t = hit.T
    hit_rows = jnp.concatenate([hit_t[:BAND], hit_t[BAND:]], axis=1).astype(BF16)

    def both(ref, r):
        return jnp.concatenate([ref[:, r, :], ref[:, r + 1, :]], axis=0)

    inv_at = both(recv0, 0)
    l1 = inv_at * (p0_at - both(recv0, 2))
    p2_part = -off_m(pm[1], *halo(0))
    part_cols = end_cols(p2_part)
    pushed = co[5, 0:BAND] * pick(hit_rows, [l1])[0]
    pm[2] = p2_part
    pm[2, 0:BAND] += pushed
    pushed_cols = jnp.concatenate(
        [end_cols(pushed), jnp.zeros((8, ROWS - BAND), F32)], axis=1
    )
    halo_send(
        1,
        p2_part[0:1] + pushed[0:1],
        p2_part[ROWS - 1 : ROWS],
        part_cols + pushed_cols,
    )
    for o in OFFSETS:
        send_to(o, send4, recv4, 4)
    p2 = pm[2]
    p2_at = sample([p2[0:BAND]])[0]
    all_arrived(send3, recv3, 3).wait_recv()
    ratio_at = both(recv3, 0)
    l2 = inv_at * (p1_at - both(recv3, 2)) - (1.0 + ratio_at) * l1
    metric_at = jnp.where(inv_at > 0.0, 1.0 / inv_at, 0.0)
    m1, m2 = metric_at * l1, metric_at * l2
    moments[2] += fold(m1 * l1)
    moments.append(fold(m1 * l2))
    moments.append(fold(m2 * l2))
    d2 = co[4] * pm[2]
    moments[3] += fold(d2 * pm[1])
    moments[4] += fold(d2 * pm[2])
    p3_ref[...] = -off_m(pm[2], *halo(1))
    p3_ref[0:BAND] += co[5, 0:BAND] * pick(hit_rows, [l2])[0]
    p3 = p3_ref[...]
    moments.append(fold(d2 * p3))
    moments.append(fold(co[4] * p3 * p3))
    l3_part = inv_at * p2_at + (1.0 - ratio_at) * l1 - (1.0 + ratio_at) * l2

    all_arrived(send1, recv1, 1).wait_recv()

    def returned(r):
        return jnp.concatenate([recv1[:, r, :], recv1[:, r + 1, :]], axis=0)

    p0_at, p1_at = pick(slot_hot_t, [returned(0), returned(2)])
    l1 = inv_l * (p0_at - fm[0])
    l2 = inv_l * (p1_at - fm[1]) - (1.0 + ratio_l) * l1
    q2 = q2_part - inv_f * l1
    q3 = -inv_f * (off_f(q2) + l2)
    fm[2] = q2
    fm[3] = l1
    fm[4] = l2
    s2 = safe * q2
    moments[3] += fold(s2 * fm[1])
    moments[4] += fold(s2 * q2)
    moments[5] += fold(s2 * q3)
    moments[6] += fold(safe * q3 * q3)
    all_arrived(send4, recv4, 4).wait_recv()
    l3 = l3_part - inv_at * both(recv4, 0)
    moments[5] += fold(m2 * l3)
    moments[6] += fold(metric_at * l3 * l3)
    rows = [jnp.sum(m, axis=0, keepdims=True) for m in moments]
    sums = jnp.sum(jnp.concatenate(rows + [jnp.zeros((1, N), F32)], axis=0), axis=1, keepdims=True)
    mine = jnp.sum(jnp.where(lane8 == sub8, sums, 0.0), axis=0, keepdims=True)
    send2[0:1] = mine
    recv2[pl.ds(me, 1), 0:1] = mine[None]
    for o in OFFSETS:
        pltpu.make_async_remote_copy(
            send2.at[0:1],
            recv2.at[me, 0:1],
            ssem.at[2],
            rsem.at[2],
            device_id=target(o),
            device_id_type=LOGICAL,
        ).start()
    all_arrived(recv2.at[:, 0:1], recv2.at[:, 0:1], 2).wait_recv()
    total = jnp.sum(fold(recv2[:, 0, :]), axis=0, keepdims=True)
    mu = [jnp.broadcast_to(total[:, i : i + 1], (1, N)) for i in range(7)]

    gram = [mu[k] + 2.0 * mu[k + 1] + mu[k + 2] for k in range(5)]
    right_side = [mu[k] + mu[k + 1] for k in range(3)]
    i0 = 1.0 / gram[0]
    l10, l20 = gram[1] * i0, gram[2] * i0
    i1 = 1.0 / (gram[2] - l10 * gram[1])
    off = gram[3] - l20 * gram[1]
    l21 = off * i1
    i2 = 1.0 / (gram[4] - l20 * gram[2] - l21 * off)
    y1 = right_side[1] - l10 * right_side[0]
    y2 = right_side[2] - l20 * right_side[0] - l21 * y1
    x2 = y2 * i2
    x1 = y1 * i1 - l21 * x2
    x0 = right_side[0] * i0 - l10 * x1 - l20 * x2
    factors[...] = jnp.concatenate([x0, x1, x2, jnp.zeros((5, N), F32)], axis=0)

    all_arrived(send0, recv0, 0).wait_send()
    all_arrived(send1, recv1, 1).wait_send()
    all_arrived(recv2.at[:, 0:1], recv2.at[:, 0:1], 2).wait_send()
    all_arrived(send3, recv3, 3).wait_send()
    all_arrived(send4, recv4, 4).wait_send()
    for i in range(7):
        edge_copy(i).wait_send()
    for phase in range(2):
        for way in range(4):
            halo_copy(phase, way).wait_send()


def combine(pm, fm, factors, out_m, out_f, out_l, om, of, ol, sem):
    x0, x1, x2 = factors[0:1], factors[1:2], factors[2:3]
    stores = [
        pltpu.make_async_copy(om, out_m, sem.at[0]),
        pltpu.make_async_copy(of, out_f, sem.at[1]),
        pltpu.make_async_copy(ol, out_l, sem.at[2]),
    ]
    om[...] = x0 * pm[0] + x1 * pm[1] + x2 * pm[2]
    stores[0].start()
    of[...] = x0 * fm[0] + x1 * fm[1] + x2 * fm[2]
    stores[1].start()
    ol[...] = x1 * fm[3] + x2 * fm[4]
    stores[2].start()
    for store in stores:
        store.wait()


def local(
    rhs_matrix,
    trans_x,
    trans_y,
    leak_matrix,
    rhs_fracture,
    trans_frac,
    store_frac,
    mortar_coef,
    block_home,
    block_len,
    mortar_cell,
    cross_cell,
    cross_partner,
    cross_trans,
):
    tile, block = (ROWS, N), (N, N)
    vmem = lambda shape, kind=F32: pltpu.VMEM(shape, kind)
    results = pl.pallas_call(
        kernel,
        out_shape=(vmem((3,) + tile), vmem((5,) + block), vmem((8, N))),
        in_specs=[pl.BlockSpec(memory_space=pl.ANY)] * 14,
        out_specs=(pl.BlockSpec(memory_space=pltpu.VMEM),) * 3,
        scratch_shapes=[vmem(tile)] * 4
        + [vmem(block)] * 4
        + [vmem((1, N), jnp.int32)] * 3
        + [vmem((2, N), jnp.int32)] * 2
        + [vmem((2, N))]
        + [
            vmem(tile),
            vmem((6,) + tile),
            vmem((N, ROWS0, N)),
            vmem((N, ROWS0, N)),
            vmem((N, ROWS1, N)),
            vmem((N, ROWS1, N)),
            vmem((8, N)),
            vmem((N, 8, N)),
            vmem((N, ROWS3, N)),
            vmem((N, ROWS3, N)),
            vmem((N, ROWS4, N)),
            vmem((N, ROWS4, N)),
            vmem((2, 2, 1, N)),
            vmem((2, 2, 1, N)),
            vmem((2, 2, 1, ROWS)),
            vmem((2, 2, 1, ROWS)),
            vmem((9, 1, N)),
            vmem((9, 1, N)),
            vmem((5, 1, ROWS)),
            vmem((5, 1, ROWS)),
            pltpu.SemaphoreType.DMA((14,)),
            pltpu.SemaphoreType.DMA((5,)),
            pltpu.SemaphoreType.DMA((5,)),
            pltpu.SemaphoreType.DMA((2, 4)),
            pltpu.SemaphoreType.DMA((2, 4)),
            pltpu.SemaphoreType.DMA((7,)),
            pltpu.SemaphoreType.DMA((7,)),
        ],
        compiler_params=pltpu.CompilerParams(
            collective_id=0, has_side_effects=True, vmem_limit_bytes=60 * 2**20
        ),
    )(
        *[
            pltpu.with_memory_space_constraint(operand, pltpu.HBM)
            for operand in (
                rhs_matrix,
                trans_x,
                trans_y,
                leak_matrix,
                rhs_fracture,
                trans_frac,
                store_frac,
                mortar_coef,
                block_home.T,
                block_len.reshape(1, N),
                mortar_cell.T,
                cross_cell.T,
                cross_partner.T,
                cross_trans.T,
            )
        ]
    )
    return pl.pallas_call(
        combine,
        out_shape=(
            jax.ShapeDtypeStruct(tile, F32),
            jax.ShapeDtypeStruct(block, F32),
            jax.ShapeDtypeStruct(block, F32),
        ),
        in_specs=[pl.BlockSpec(memory_space=pltpu.VMEM)] * 3,
        out_specs=(pl.BlockSpec(memory_space=pl.ANY),) * 3,
        scratch_shapes=[vmem(tile), vmem(block), vmem(block), pltpu.SemaphoreType.DMA((3,))],
    )(*[pltpu.with_memory_space_constraint(result, pltpu.VMEM) for result in results])


def solution(mesh):
    tiles, blocks = P("gx", "gy"), P(("gx", "gy"), None)
    return jax.shard_map(
        local,
        mesh=mesh,
        in_specs=(tiles,) * 4 + (blocks,) * 5 + (P(("gx", "gy")),) + (blocks,) * 4,
        out_specs=(tiles, blocks, blocks),
        check_vma=False,
    )
```

```python
import jax
import jax.numpy as jnp
from jax import lax
from jax.experimental import pallas as pl
from jax.experimental.pallas import tpu as pltpu
from jax.sharding import PartitionSpec as P

LOGICAL = pl.DeviceIdType.LOGICAL
F32 = jnp.float32
BF16 = jnp.bfloat16

N = 128
ROWS = 256
BAND = 64
ROWS0 = 5
ROWS1 = 4
ROWS3 = 4
ROWS4 = 2

HOPS = (0, 1, 2, 1)
OFFSETS = sorted(
    (
        (dy, dc, dz, dx)
        for dy in range(4)
        for dc in range(2)
        for dz in range(4)
        for dx in range(4)
        if (dy, dc, dz, dx) != (0, 0, 0, 0)
    ),
    key=lambda o: (-(2 * (HOPS[o[0]] + HOPS[o[2]] + HOPS[o[3]]) + o[1]), o),
)


def split(value):
    high = value.astype(BF16)
    return [high, (value - high.astype(F32)).astype(BF16)]


def pick(hot, fields):
    if hot.shape[1] == N:
        columns = jnp.concatenate(fields, axis=1)
        stacked = jnp.concatenate(split(columns), axis=0)
        out = jnp.dot(
            jnp.concatenate([hot] * 2, axis=1), stacked, preferred_element_type=F32
        )
        return [out[:, N * i : N * (i + 1)] for i in range(len(fields))]
    parts = [part for field in fields for part in split(field)]
    out = jnp.dot(hot, jnp.concatenate(parts, axis=1), preferred_element_type=F32)
    n = fields[0].shape[1]
    return [
        out[:, 2 * n * i : 2 * n * i + n] + out[:, 2 * n * i + n : 2 * n * i + 2 * n]
        for i in range(len(fields))
    ]


def fold(value):
    total = value[0:8]
    for i in range(8, value.shape[0], 8):
        total = total + value[i : i + 8]
    return total


def kernel(
    rhs_m_hbm,
    tx_hbm,
    ty_hbm,
    leak_hbm,
    rhs_f_hbm,
    tf_hbm,
    sf_hbm,
    coef_hbm,
    home_hbm,
    len_hbm,
    mcell_hbm,
    cc_hbm,
    cp_hbm,
    ct_hbm,
    pm,
    fm,
    factors,
    rhs_m,
    tx,
    ty,
    leak,
    rhs_f,
    tf,
    sf,
    coef,
    home,
    blen,
    mcell,
    cc,
    cp,
    ct,
    p3_ref,
    co,
    send0,
    recv0,
    send1,
    recv1,
    send2,
    recv2,
    send3,
    recv3,
    send4,
    recv4,
    hsend_r,
    hrecv_r,
    hsend_c,
    hrecv_c,
    esend_r,
    erecv_r,
    esend_c,
    erecv_c,
    in_sem,
    ssem,
    rsem,
    hs_sem,
    hr_sem,
    es_sem,
    er_sem,
):
    gx = lax.axis_index("gx")
    gy = lax.axis_index("gy")
    me = gx * 16 + gy

    pairs = [
        (len_hbm, blen),
        (home_hbm, home),
        (mcell_hbm, mcell),
        (cc_hbm, cc),
        (cp_hbm, cp),
        (ct_hbm, ct),
        (tf_hbm, tf),
        (sf_hbm, sf),
        (rhs_f_hbm, rhs_f),
        (coef_hbm, coef),
        (tx_hbm, tx),
        (ty_hbm, ty),
        (leak_hbm, leak),
        (rhs_m_hbm, rhs_m),
    ]
    loads = [pltpu.make_async_copy(a, b, in_sem.at[i]) for i, (a, b) in enumerate(pairs)]
    for load in loads:
        load.start()

    ys = [lax.rem(gx // 2 + d, 4) * 32 for d in range(4)]
    cs = [lax.rem(gx + d, 2) * 16 for d in range(2)]
    zs = [lax.rem(gy // 4 + d, 4) * 4 for d in range(4)]
    xs = [lax.rem(gy + d, 4) for d in range(4)]

    def target(o):
        return (ys[o[0]] + cs[o[1]]) + (zs[o[2]] + xs[o[3]])

    barrier = pltpu.get_barrier_semaphore()
    for o in OFFSETS:
        pl.semaphore_signal(barrier, inc=1, device_id=target(o), device_id_type=LOGICAL)

    below = lax.rem(gx + 1, 8) * 16 + gy
    above = lax.rem(gx + 7, 8) * 16 + gy
    right = gx * 16 + lax.rem(gy + 1, 16)
    left = gx * 16 + lax.rem(gy + 15, 16)
    below_right = lax.rem(gx + 1, 8) * 16 + lax.rem(gy + 1, 16)
    above_right = lax.rem(gx + 7, 8) * 16 + lax.rem(gy + 1, 16)
    below_left = lax.rem(gx + 1, 8) * 16 + lax.rem(gy + 15, 16)
    has_above = jnp.where(gx > 0, 1.0, 0.0).astype(F32)
    has_below = jnp.where(gx < 7, 1.0, 0.0).astype(F32)
    has_left = jnp.where(gy > 0, 1.0, 0.0).astype(F32)
    has_right = jnp.where(gy < 15, 1.0, 0.0).astype(F32)

    lane = lax.broadcasted_iota(jnp.int32, (N, N), 1)
    row = lax.broadcasted_iota(jnp.int32, (N, N), 0)

    for load in loads[:6]:
        load.wait()
    lanef = lane.astype(F32)
    len_row = blen[...].astype(F32)
    cp_row = cp[...]
    pb_row = cp_row // N
    pc_row = cp_row - pb_row * N
    table = jnp.concatenate(
        [
            len_row,
            cc[...].astype(F32),
            pb_row.astype(F32),
            pc_row.astype(F32),
            ct[...],
            jnp.zeros((N - 9, N), F32),
        ],
        axis=0,
    ).T
    len_col = table[:, 0:1]
    own_hot = [lanef == table[:, 1 + k : 2 + k] for k in range(2)]
    part_rows = [lanef == table[:, 3 + k : 4 + k] for k in range(2)]
    part_hot = [lanef == table[:, 5 + k : 6 + k] for k in range(2)]
    weight = []
    for k in range(2):
        part_len = jnp.sum(jnp.where(part_rows[k], len_row, 0.0), axis=1, keepdims=True)
        live = (table[:, 1 + k : 2 + k] < len_col) & (table[:, 5 + k : 6 + k] < part_len)
        weight.append(jnp.where(live, table[:, 7 + k : 8 + k], 0.0))
    gather_hot = jnp.concatenate([jnp.where(h, 1.0, 0.0) for h in part_rows], axis=0).astype(BF16)
    spread_hot = jnp.concatenate(
        [jnp.where(row == pb_row[k : k + 1], 1.0, 0.0) for k in range(2)], axis=1
    ).astype(BF16)

    def spread(own_values, part_values):
        pieces = jnp.concatenate(
            [jnp.where(part_hot[k], part_values[k], 0.0) for k in range(2)], axis=0
        )
        out = pick(spread_hot, [pieces])[0]
        for k in range(2):
            out = out + jnp.where(own_hot[k], own_values[k], 0.0)
        return out

    for load in loads[6:10]:
        load.wait()
    mask = jnp.where(lanef < len_col, 1.0, 0.0)
    face = jnp.where(lanef + 1.0 < len_col, tf[...], 0.0)
    face_prev = pltpu.roll(face, 1, 1)
    diag_f = sf[...] * mask + face + face_prev + spread(weight, weight)
    safe = diag_f + 1.0 - mask
    inv_f = mask / safe
    metric_l = 1.0 / coef[...] + 1.0 / safe
    inv_l = mask / metric_l
    ratio_l = inv_l / coef[...]
    q0 = inv_f * rhs_f[...]

    def off_f(q):
        rows = pick(gather_hot, [q])[0]
        part = [
            jnp.sum(jnp.where(part_hot[k], rows[k * N : k * N + N], 0.0), axis=1, keepdims=True)
            for k in range(2)
        ]
        own = [jnp.sum(jnp.where(own_hot[k], q, 0.0), axis=1, keepdims=True) for k in range(2)]
        crossing = spread(
            [weight[k] * part[k] for k in range(2)], [weight[k] * own[k] for k in range(2)]
        )
        return face * pltpu.roll(q, N - 1, 1) + face_prev * pltpu.roll(q, 1, 1) + crossing

    q1 = -inv_f * off_f(q0)

    home_hit = row == home[...]
    first = jnp.min(jnp.where(home_hit, lanef, 1e3), axis=1, keepdims=True)
    last = jnp.max(jnp.where(home_hit, lanef, -1.0), axis=1, keepdims=True)
    slots = [
        jnp.where(lanef == first, 1.0, 0.0),
        jnp.where((lanef == last) & (last > first), 1.0, 0.0),
    ]
    mcell_row = mcell[...].astype(F32)
    cells = [jnp.sum(s * mcell_row, axis=1, keepdims=True) for s in slots]
    slot_hot = jnp.concatenate(slots, axis=0).astype(BF16)
    q2_part = -inv_f * off_f(q1)
    packed = pick(slot_hot, [inv_l, q0, ratio_l, q1, q2_part])
    for i, value in enumerate(packed[:2]):
        send0[:, 2 * i, :] = value[:N]
        send0[:, 2 * i + 1, :] = value[N:]
    send0[:, 4, :] = jnp.where(lane < BAND, cells[0], cells[1])
    send4[:, 0, :] = packed[4][:N]
    send4[:, 1, :] = packed[4][N:]
    for i, value in enumerate(packed[2:4]):
        send3[:, 2 * i, :] = value[:N]
        send3[:, 2 * i + 1, :] = value[N:]
    recv0[pl.ds(me, 1)] = send0[pl.ds(me, 1)]
    recv3[pl.ds(me, 1)] = send3[pl.ds(me, 1)]
    recv4[pl.ds(me, 1)] = send4[pl.ds(me, 1)]

    fm[0] = q0
    fm[1] = q1

    for load in loads[10:]:
        load.wait()
    sub8 = lax.broadcasted_iota(jnp.int32, (8, N), 0)
    lane8 = lax.broadcasted_iota(jnp.int32, (8, N), 1)
    ends = jnp.where(
        ((sub8 == 0) & (lane8 == 0)) | ((sub8 == 1) & (lane8 == N - 1)), 1.0, 0.0
    ).astype(BF16)

    def end_cols(field):
        return lax.dot_general(
            jnp.concatenate([ends] * 2, axis=1),
            jnp.concatenate(split(field), axis=1),
            (((1,), (1,)), ((), ())),
            preferred_element_type=F32,
        )

    def halo_copy(phase, way):
        device = (below, above, right, left)[way]
        send, recv = (hsend_r, hrecv_r) if way < 2 else (hsend_c, hrecv_c)
        return pltpu.make_async_remote_copy(
            send.at[phase, way % 2],
            recv.at[phase, way % 2],
            hs_sem.at[phase, way],
            hr_sem.at[phase, way],
            device_id=device,
            device_id_type=LOGICAL,
        )

    def halo_send(phase, first, last, cols):
        hsend_r[phase, 0] = last
        hsend_r[phase, 1] = first
        hsend_c[phase, 0] = cols[1:2]
        hsend_c[phase, 1] = cols[0:1]
        for way in range(4):
            halo_copy(phase, way).start()

    def as_cols(rows):
        cols = jnp.concatenate(rows + [jnp.zeros((8 - len(rows), ROWS), F32)], axis=0).T
        return [cols[:, k : k + 1] for k in range(len(rows))]

    row_m = lax.broadcasted_iota(jnp.int32, (ROWS, N), 0)
    lane_m = lax.broadcasted_iota(jnp.int32, (ROWS, N), 1)

    def off_m(p, top, bottom, before, after):
        up = jnp.where(row_m == 0, top, pltpu.roll(p, 1, 0))
        down = jnp.where(row_m == ROWS - 1, bottom, pltpu.roll(p, ROWS - 1, 0))
        lft = jnp.where(lane_m == 0, before, pltpu.roll(p, 1, 1))
        rgt = jnp.where(lane_m == N - 1, after, pltpu.roll(p, N - 1, 1))
        return co[0] * down + co[1] * up + co[2] * rgt + co[3] * lft

    def halo(phase):
        for way in range(4):
            halo_copy(phase, way).wait_recv()
        before, after = as_cols([hrecv_c[phase, 0] * has_left, hrecv_c[phase, 1] * has_right])
        return hrecv_r[phase, 0] * has_above, hrecv_r[phase, 1] * has_below, before, after

    tx_up = jnp.where(row_m == 0, 0.0, pltpu.roll(tx[...], 1, 0))
    ty_left = jnp.where(lane_m == 0, 0.0, pltpu.roll(ty[...], 1, 1))
    partial = leak[...] + tx[...] + tx_up + ty[...] + ty_left
    esend_r[0] = tx[ROWS - 1 : ROWS]
    esend_r[1] = rhs_m[ROWS - 1 : ROWS]
    esend_r[2] = partial[ROWS - 1 : ROWS]
    esend_r[3] = rhs_m[0:1]
    esend_r[4] = partial[0:1]
    esend_r[5] = tx[ROWS - 1 : ROWS]
    esend_r[6] = ty[ROWS - 1 : ROWS]
    esend_r[7] = ty[0:1]
    esend_r[8] = tx[ROWS - 1 : ROWS]
    ty_cols, rhs_cols, partial_cols = end_cols(ty[...]), end_cols(rhs_m[...]), end_cols(partial)
    esend_c[0] = ty_cols[1:2]
    esend_c[1] = rhs_cols[1:2]
    esend_c[2] = partial_cols[1:2]
    esend_c[3] = rhs_cols[0:1]
    esend_c[4] = partial_cols[0:1]

    def edge_copy(i):
        send, recv, start, count, device = (
            (esend_r, erecv_r, 0, 3, below),
            (esend_r, erecv_r, 3, 2, above),
            (esend_r, erecv_r, 5, 2, below_right),
            (esend_r, erecv_r, 7, 1, above_right),
            (esend_r, erecv_r, 8, 1, below_left),
            (esend_c, erecv_c, 0, 3, right),
            (esend_c, erecv_c, 3, 2, left),
        )[i]
        return pltpu.make_async_remote_copy(
            send.at[pl.ds(start, count)],
            recv.at[pl.ds(start, count)],
            es_sem.at[i],
            er_sem.at[i],
            device_id=device,
            device_id_type=LOGICAL,
        )

    pl.semaphore_wait(barrier, N - 1)
    for i in (2, 3, 4, 0, 1, 5, 6):
        edge_copy(i).start()

    def send_to(o, send, recv, i):
        t = target(o)
        pltpu.make_async_remote_copy(
            send.at[t],
            recv.at[me],
            ssem.at[i],
            rsem.at[i],
            device_id=t,
            device_id_type=LOGICAL,
        ).start()

    for o in OFFSETS:
        send_to(o, send0, recv0, 0)

    for i in range(7):
        edge_copy(i).wait_recv()
    lane_1 = lax.broadcasted_iota(jnp.int32, (1, N), 1)

    def corner(value, factor):
        return jnp.where(lane_1 == 0, value, 0.0) * factor

    def corner_col(value, factor):
        return jnp.concatenate([corner(value, factor), jnp.zeros((1, N), F32)], axis=1)

    diag_above = erecv_r[2] + corner(pltpu.roll(erecv_r[6], 1, 1), has_left)
    diag_below = erecv_r[4] + tx[ROWS - 1 : ROWS] + corner(pltpu.roll(erecv_r[7], 1, 1), has_left)
    diag_left = erecv_c[2] + corner_col(pltpu.roll(erecv_r[5], 1, 1), has_above)
    diag_right = erecv_c[4] + esend_c[0] + corner_col(erecv_r[8], has_above)
    p0_above = erecv_r[1] / diag_above * has_above
    p0_below = erecv_r[3] / diag_below * has_below
    ty_col, p0_left, p0_right = as_cols(
        [
            erecv_c[0] * has_left,
            erecv_c[1] / diag_left * has_left,
            erecv_c[3] / diag_right * has_right,
        ]
    )
    tx_prev = jnp.where(row_m == 0, erecv_r[0] * has_above, pltpu.roll(tx[...], 1, 0))
    ty_prev = jnp.where(lane_m == 0, ty_col, pltpu.roll(ty[...], 1, 1))
    diag_m = leak[...] + tx[...] + tx_prev + ty[...] + ty_prev
    inv_m = 1.0 / diag_m
    pm[0] = rhs_m[...] * inv_m
    co[0] = tx[...] * inv_m
    co[1] = tx_prev * inv_m
    co[2] = ty[...] * inv_m
    co[3] = ty_prev * inv_m
    co[4] = diag_m
    co[5] = inv_m
    p1 = -off_m(pm[0], p0_above, p0_below, p0_left, p0_right)
    halo_send(0, p1[0:1], p1[ROWS - 1 : ROWS], end_cols(p1))
    pm[1] = p1
    for o in OFFSETS:
        send_to(o, send3, recv3, 3)

    slot_hot_t = jnp.concatenate([s.T for s in slots], axis=1).astype(BF16)
    dm = co[4]
    moments = [
        fold(dm * pm[0] * pm[0]) + fold(safe * fm[0] * fm[0]),
        fold(dm * pm[0] * pm[1]) + fold(safe * fm[0] * fm[1]),
        fold(dm * pm[1] * pm[1]) + fold(safe * fm[1] * fm[1]),
    ]

    def all_arrived(send, recv, i):
        return pltpu.make_async_remote_copy(
            send.at[pl.ds(0, N - 1)],
            recv.at[pl.ds(0, N - 1)],
            ssem.at[i],
            rsem.at[i],
            device_id=right,
            device_id_type=LOGICAL,
        )

    all_arrived(send0, recv0, 0).wait_recv()
    lane_band = jnp.where(lane < BAND, lane, lane - BAND).astype(F32)
    hit = jnp.where(recv0[:, 4, :] == lane_band, 1.0, 0.0)
    hit_slots = jnp.concatenate(
        [jnp.where(lane < BAND, hit, 0.0), jnp.where(lane < BAND, 0.0, hit)], axis=0
    ).astype(BF16)

    def sample(fields):
        return pick(hit_slots, [jnp.concatenate([f, f], axis=0) for f in fields])

    p0_at, p1_at = sample([pm[0, 0:BAND], pm[1, 0:BAND]])
    for i, value in enumerate((p0_at, p1_at)):
        send1[:, 2 * i, :] = value[:N]
        send1[:, 2 * i + 1, :] = value[N:]
    recv1[pl.ds(me, 1)] = send1[pl.ds(me, 1)]
    for o in OFFSETS:
        send_to(o, send1, recv1, 1)

    hit_t = hit.T
    hit_rows = jnp.concatenate([hit_t[:BAND], hit_t[BAND:]], axis=1).astype(BF16)

    def both(ref, r):
        return jnp.concatenate([ref[:, r, :], ref[:, r + 1, :]], axis=0)

    inv_at = both(recv0, 0)
    l1 = inv_at * (p0_at - both(recv0, 2))
    p2_part = -off_m(pm[1], *halo(0))
    part_cols = end_cols(p2_part)
    pushed = co[5, 0:BAND] * pick(hit_rows, [l1])[0]
    pm[2] = p2_part
    pm[2, 0:BAND] += pushed
    pushed_cols = jnp.concatenate(
        [end_cols(pushed), jnp.zeros((8, ROWS - BAND), F32)], axis=1
    )
    halo_send(
        1,
        p2_part[0:1] + pushed[0:1],
        p2_part[ROWS - 1 : ROWS],
        part_cols + pushed_cols,
    )
    for o in OFFSETS:
        send_to(o, send4, recv4, 4)
    p2 = pm[2]
    p2_at = sample([p2[0:BAND]])[0]
    all_arrived(send3, recv3, 3).wait_recv()
    ratio_at = both(recv3, 0)
    l2 = inv_at * (p1_at - both(recv3, 2)) - (1.0 + ratio_at) * l1
    metric_at = jnp.where(inv_at > 0.0, 1.0 / inv_at, 0.0)
    m1, m2 = metric_at * l1, metric_at * l2
    moments[2] += fold(m1 * l1)
    moments.append(fold(m1 * l2))
    moments.append(fold(m2 * l2))
    d2 = co[4] * pm[2]
    moments[3] += fold(d2 * pm[1])
    moments[4] += fold(d2 * pm[2])
    p3_ref[...] = -off_m(pm[2], *halo(1))
    p3_ref[0:BAND] += co[5, 0:BAND] * pick(hit_rows, [l2])[0]
    p3 = p3_ref[...]
    moments.append(fold(d2 * p3))
    moments.append(fold(co[4] * p3 * p3))
    l3_part = inv_at * p2_at + (1.0 - ratio_at) * l1 - (1.0 + ratio_at) * l2

    all_arrived(send1, recv1, 1).wait_recv()

    def returned(r):
        return jnp.concatenate([recv1[:, r, :], recv1[:, r + 1, :]], axis=0)

    p0_at, p1_at = pick(slot_hot_t, [returned(0), returned(2)])
    l1 = inv_l * (p0_at - fm[0])
    l2 = inv_l * (p1_at - fm[1]) - (1.0 + ratio_l) * l1
    q2 = q2_part - inv_f * l1
    q3 = -inv_f * (off_f(q2) + l2)
    fm[2] = q2
    fm[3] = l1
    fm[4] = l2
    s2 = safe * q2
    moments[3] += fold(s2 * fm[1])
    moments[4] += fold(s2 * q2)
    moments[5] += fold(s2 * q3)
    moments[6] += fold(safe * q3 * q3)
    all_arrived(send4, recv4, 4).wait_recv()
    l3 = l3_part - inv_at * both(recv4, 0)
    moments[5] += fold(m2 * l3)
    moments[6] += fold(metric_at * l3 * l3)
    rows = [jnp.sum(m, axis=0, keepdims=True) for m in moments]
    sums = jnp.sum(jnp.concatenate(rows + [jnp.zeros((1, N), F32)], axis=0), axis=1, keepdims=True)
    mine = jnp.sum(jnp.where(lane8 == sub8, sums, 0.0), axis=0, keepdims=True)
    send2[0:1] = mine
    recv2[pl.ds(me, 1), 0:1] = mine[None]
    for o in OFFSETS:
        pltpu.make_async_remote_copy(
            send2.at[0:1],
            recv2.at[me, 0:1],
            ssem.at[2],
            rsem.at[2],
            device_id=target(o),
            device_id_type=LOGICAL,
        ).start()
    all_arrived(recv2.at[:, 0:1], recv2.at[:, 0:1], 2).wait_recv()
    total = jnp.sum(fold(recv2[:, 0, :]), axis=0, keepdims=True)
    mu = [jnp.broadcast_to(total[:, i : i + 1], (1, N)) for i in range(7)]

    gram = [mu[k] + 2.0 * mu[k + 1] + mu[k + 2] for k in range(5)]
    right_side = [mu[k] + mu[k + 1] for k in range(3)]
    i0 = 1.0 / gram[0]
    l10, l20 = gram[1] * i0, gram[2] * i0
    i1 = 1.0 / (gram[2] - l10 * gram[1])
    off = gram[3] - l20 * gram[1]
    l21 = off * i1
    i2 = 1.0 / (gram[4] - l20 * gram[2] - l21 * off)
    y1 = right_side[1] - l10 * right_side[0]
    y2 = right_side[2] - l20 * right_side[0] - l21 * y1
    x2 = y2 * i2
    x1 = y1 * i1 - l21 * x2
    x0 = right_side[0] * i0 - l10 * x1 - l20 * x2
    factors[...] = jnp.concatenate([x0, x1, x2, jnp.zeros((5, N), F32)], axis=0)

    all_arrived(send0, recv0, 0).wait_send()
    all_arrived(send1, recv1, 1).wait_send()
    all_arrived(recv2.at[:, 0:1], recv2.at[:, 0:1], 2).wait_send()
    all_arrived(send3, recv3, 3).wait_send()
    all_arrived(send4, recv4, 4).wait_send()
    for i in range(7):
        edge_copy(i).wait_send()
    for phase in range(2):
        for way in range(4):
            halo_copy(phase, way).wait_send()


def combine(pm, fm, factors, out_m, out_f, out_l, om, of, ol, sem):
    x0, x1, x2 = factors[0:1], factors[1:2], factors[2:3]
    stores = [
        pltpu.make_async_copy(om, out_m, sem.at[0]),
        pltpu.make_async_copy(of, out_f, sem.at[1]),
        pltpu.make_async_copy(ol, out_l, sem.at[2]),
    ]
    om[...] = x0 * pm[0] + x1 * pm[1] + x2 * pm[2]
    stores[0].start()
    of[...] = x0 * fm[0] + x1 * fm[1] + x2 * fm[2]
    stores[1].start()
    ol[...] = x1 * fm[3] + x2 * fm[4]
    stores[2].start()
    for store in stores:
        store.wait()


def local(
    rhs_matrix,
    trans_x,
    trans_y,
    leak_matrix,
    rhs_fracture,
    trans_frac,
    store_frac,
    mortar_coef,
    block_home,
    block_len,
    mortar_cell,
    cross_cell,
    cross_partner,
    cross_trans,
):
    tile, block = (ROWS, N), (N, N)
    vmem = lambda shape, kind=F32: pltpu.VMEM(shape, kind)
    results = pl.pallas_call(
        kernel,
        out_shape=(vmem((3,) + tile), vmem((5,) + block), vmem((8, N))),
        in_specs=[pl.BlockSpec(memory_space=pl.ANY)] * 14,
        out_specs=(pl.BlockSpec(memory_space=pltpu.VMEM),) * 3,
        scratch_shapes=[vmem(tile)] * 4
        + [vmem(block)] * 4
        + [vmem((1, N), jnp.int32)] * 3
        + [vmem((2, N), jnp.int32)] * 2
        + [vmem((2, N))]
        + [
            vmem(tile),
            vmem((6,) + tile),
            vmem((N, ROWS0, N)),
            vmem((N, ROWS0, N)),
            vmem((N, ROWS1, N)),
            vmem((N, ROWS1, N)),
            vmem((8, N)),
            vmem((N, 8, N)),
            vmem((N, ROWS3, N)),
            vmem((N, ROWS3, N)),
            vmem((N, ROWS4, N)),
            vmem((N, ROWS4, N)),
            vmem((2, 2, 1, N)),
            vmem((2, 2, 1, N)),
            vmem((2, 2, 1, ROWS)),
            vmem((2, 2, 1, ROWS)),
            vmem((9, 1, N)),
            vmem((9, 1, N)),
            vmem((5, 1, ROWS)),
            vmem((5, 1, ROWS)),
            pltpu.SemaphoreType.DMA((14,)),
            pltpu.SemaphoreType.DMA((5,)),
            pltpu.SemaphoreType.DMA((5,)),
            pltpu.SemaphoreType.DMA((2, 4)),
            pltpu.SemaphoreType.DMA((2, 4)),
            pltpu.SemaphoreType.DMA((7,)),
            pltpu.SemaphoreType.DMA((7,)),
        ],
        compiler_params=pltpu.CompilerParams(
            collective_id=0, has_side_effects=True, vmem_limit_bytes=60 * 2**20
        ),
    )(
        *[
            pltpu.with_memory_space_constraint(operand, pltpu.HBM)
            for operand in (
                rhs_matrix,
                trans_x,
                trans_y,
                leak_matrix,
                rhs_fracture,
                trans_frac,
                store_frac,
                mortar_coef,
                block_home.T,
                block_len.reshape(1, N),
                mortar_cell.T,
                cross_cell.T,
                cross_partner.T,
                cross_trans.T,
            )
        ]
    )
    return pl.pallas_call(
        combine,
        out_shape=(
            jax.ShapeDtypeStruct(tile, F32),
            jax.ShapeDtypeStruct(block, F32),
            jax.ShapeDtypeStruct(block, F32),
        ),
        in_specs=[pl.BlockSpec(memory_space=pltpu.VMEM)] * 3,
        out_specs=(pl.BlockSpec(memory_space=pl.ANY),) * 3,
        scratch_shapes=[vmem(tile), vmem(block), vmem(block), pltpu.SemaphoreType.DMA((3,))],
    )(*[pltpu.with_memory_space_constraint(result, pltpu.VMEM) for result in results])


def solution(mesh):
    tiles, blocks = P("gx", "gy"), P(("gx", "gy"), None)
    return jax.shard_map(
        local,
        mesh=mesh,
        in_specs=(tiles,) * 4 + (blocks,) * 5 + (P(("gx", "gy")),) + (blocks,) * 4,
        out_specs=(tiles, blocks, blocks),
        check_vma=False,
    )
```
